32 devices in a mesh: dp: 4 (over x, core), expert: 8 (over z, y).
Axes of the slice: x: 2, y: 2, z: 4, core: 2. Of those that a mesh axis runs over, the one named last changes fastest.
Arguments:
- tokens: bfloat16 [16384, 1280], P(('dp', 'expert')), may hold values from -6 to 6
- w_qkv: bfloat16 [1280, 3840], P(('dp', 'expert')), may hold values from -0.15625 to 0.15625
- w_attn_out: bfloat16 [1280, 1280], P(('dp', 'expert')), may hold values from -1.25 to 1.25
- w_shared_in: bfloat16 [1280, 1792], P(('dp', 'expert')), may hold values from -0.15625 to 0.15625
- w_shared_out: bfloat16 [896, 1280], P(('dp', 'expert')), may hold values from -0.375 to 0.375
- gain_attn: bfloat16 [1280], P(('dp', 'expert')), may hold values from 0.5 to 1.5
- gain_ffn: bfloat16 [1280], P(('dp', 'expert')), may hold values from 0.5 to 1.5
- w_expert_in: bfloat16 [16, 1280, 1792], P('expert'), may hold values from -0.15625 to 0.15625
- w_expert_out: bfloat16 [16, 896, 1280], P('expert'), may hold values from -0.75 to 0.75
- route_ids: int32 [16384, 6], P(('dp', 'expert')), may hold values from 0 to 15, all different within a row; in each aligned block of 512 rows (0 to 511, 512 to 1023, ...) at most 240 rows name the same one
- route_gates: float32 [16384, 6], P(('dp', 'expert')), may hold values from 0.08 to 0.25
- seq_lengths: int32 [32], P(('dp', 'expert')), may hold values from 1 to 512, 12288 in all
- cotangent: bfloat16 [16384, 1280], P(('dp', 'expert')), may hold values from -6 to 6
Outputs:
- block_out: bfloat16 [16384, 1280], P(('dp', 'expert'))
- grad_tokens: float32 [16384, 1280], P(('dp', 'expert'))
- grad_qkv: float32 [1280, 3840], P(('dp', 'expert'))
- grad_attn_out: float32 [1280, 1280], P(('dp', 'expert'))
- grad_shared_in: float32 [1280, 1792], P(('dp', 'expert'))
- grad_shared_out: float32 [896, 1280], P(('dp', 'expert'))
- grad_gain_attn: float32 [1280], P(('dp', 'expert'))
- grad_gain_ffn: float32 [1280], P(('dp', 'expert'))
- grad_expert_in: float32 [16, 1280, 1792], P('expert')
- grad_expert_out: float32 [16, 896, 1280], P('expert')
- expert_counts: int32 [16], replicated
The draws below stay inside these ranges and needn't reach their ends.
Inputs may be any that keep to these rules, and one draw needn't show every extreme that they name: `route_ids`: each row names 6 different experts. Within the rows of one sequence no expert is named more than 240 times, and in some sequence some expert is named exactly 240 times. `seq_lengths`: live tokens are the first ones of a sequence; some sequence is full.
All inputs are finite; a program needn't handle non-finite values. No bound on the sum of `seq_lengths` on one device may be relied on, other than what follows from the above.
Results may differ from the reference program's by a relative error of at most 0.014.
Values may be sent and summed in bfloat16 or wider, within the bound.
No kernel may reach another device: no remote copies, remote signals or barrier semaphores. Data moves between devices by JAX's collectives and lax.ppermute only.
A program may use at most 320 MiB of HBM per device.

```python
import math
import jax
import jax.numpy as jnp
import numpy as np
from jax import lax

D = 1280
HEADS = 10
HEAD_DIM = 128
FF = 896
SFF = 896
TOP = 6
TOK_DEV = 512
EXPERTS = 16
CAP = 240
SEQS = 32
TOKENS = 16384


def strengthened(values, key, source, target, blocks, factor):
    owner, partner = [(jnp.arange(values.shape[dim]) // (values.shape[dim] // blocks)).reshape([-1 if axis == dim else 1 for axis in range(values.ndim)]) for dim in (source, target)]
    chosen = jax.random.permutation(key, blocks)[partner]
    strong = (owner == chosen) | (owner == (partner + blocks // 2) % blocks)
    return jnp.where(strong, factor * values, values)


def shard_levels(own_key, extent, pieces, low, top_value):
    gain = 1.0
    for position, shards_of in pieces:
        draws = jax.random.uniform(jax.random.fold_in(jax.random.fold_in(own_key, 6), position), (shards_of,), jnp.float32, low / len(pieces), top_value / len(pieces))
        gain = gain * jnp.repeat(jnp.exp(draws), extent[position] // shards_of).reshape((-1,) + (1,) * (len(extent) - 1 - position))
    return gain


def split_up(amount, total, bound, slope):
    portions = [(1 << 20) // math.isqrt(rank ** slope) + 1 for rank in range(2, amount + 1)]
    spare, given = total - bound - (amount - 1), [1] * (amount - 1)
    while spare > 0:
        movable = [i for i in range(amount - 1) if given[i] < bound]
        pool, remaining = sum([portions[i] for i in movable]), spare
        for i in movable:
            addition = min(bound - given[i], max(1, remaining * portions[i] // pool), spare)
            given[i] = given[i] + addition
            spare = spare - addition
    return np.array([bound] + given)


def ragged_sizes(stream_key, amount, total, reach, slope):
    if amount == 2:
        one = jax.random.randint(stream_key, (), max(1, total - reach), min(reach, total - 1) + 1)
        return jnp.stack([one, total - one])
    sizes = jnp.asarray(split_up(amount, total, reach, slope), jnp.int32)
    twos = (amount - 1) // 2
    donor, receiver = sizes[1:1 + 2 * twos:2], sizes[2:2 + 2 * twos:2]
    margin = jnp.minimum(donor - 1, reach - receiver)
    passed = jax.random.randint(jax.random.fold_in(stream_key, 1), (twos,), 0, 1 << 20) % (margin + 1)
    sizes = sizes.at[1:1 + 2 * twos:2].set(donor - passed).at[2:2 + 2 * twos:2].set(receiver + passed)
    return sizes[jax.random.permutation(jax.random.fold_in(stream_key, 2), amount)]


def shared_out(stream_key, own, number, rows, amount, top, most, slope):
    sequence = jax.random.permutation(stream_key, amount)
    crowded, usual = load_shares(amount, rows * top, most, slope, True), load_shares(amount, rows * top, most, slope, False)
    places = jnp.arange(amount)

    def named(tallies, rotation):
        used = int((tallies > 0).sum())
        fixed = max(1, used // 4)
        passed = fixed + (places - fixed + rotation * (used - fixed)) % max(1, amount - fixed)
        return jnp.zeros((amount,), jnp.int32).at[sequence[jnp.where(places < fixed, places, passed)]].set(jnp.asarray(tallies, jnp.int32))

    tallies = jnp.where(number % 4 == 0, named(crowded, number // 4), named(usual, number - number // 4 - 1))
    mixed = jax.random.permutation(jax.random.fold_in(own, 3), amount)
    source_of, receiver = mixed[0:amount // 2 * 2:2], mixed[1:amount // 2 * 2:2]
    room = jnp.minimum(tallies[source_of] - 1, most - tallies[receiver]) // 2
    room = jnp.where((source_of == sequence[0]) | (receiver == sequence[0]) | (tallies[receiver] == 0), 0, jnp.maximum(room, 0))
    passed = jax.random.randint(jax.random.fold_in(own, 4), (amount // 2,), 0, 1 << 20) % (room + 1)
    tallies = tallies.at[source_of].add(-passed).at[receiver].add(passed)
    members = jnp.searchsorted(jnp.cumsum(tallies), jnp.arange(rows * top), side="right").astype(jnp.int32)
    table = members.reshape(top, rows).T
    table = table[jax.random.permutation(jax.random.fold_in(own, 1), rows)]
    rotation = jax.random.randint(jax.random.fold_in(own, 2), (rows, 1), 0, top)
    return jnp.take_along_axis(table, (jnp.arange(top)[None, :] + rotation) % top, axis=1)


def load_shares(number_of, total, reach, lean, full):
    weights = [(1 << 20) // math.isqrt(rank ** lean) + 1 for rank in range(1, number_of + 1)]
    largest = reach if full else min(reach, max(-(-total // number_of), total * weights[0] // sum(weights)))
    least = 1 if total - largest >= number_of - 1 else 0
    holding, surplus = [largest] + [least] * (number_of - 1), total - largest - least * (number_of - 1)
    while surplus > 0:
        movable = [i for i in range(1, number_of) if holding[i] < largest] or [i for i in range(1, number_of) if holding[i] < reach]
        whole, remaining = sum([weights[i] for i in movable]), surplus
        for i in movable:
            addition = min(reach - holding[i], max(1, remaining * weights[i] // whole), surplus)
            holding[i] = holding[i] + addition
            surplus = surplus - addition
    return np.array(holding)


def noise(rng, dims, spread, bound, split=(), kind=jnp.bfloat16):
    values = jax.random.normal(rng, dims, jnp.float32) * spread
    if len(split) > 0:
        values = shard_levels(rng, dims, split, -0.22, 0.18) * values
    return jnp.clip(values, min=-bound, max=bound).astype(kind)


def gaussian_with(key, dims, deviation, bound, split, heavy, kind=jnp.bfloat16):
    entries = deviation * jax.random.normal(key, dims, jnp.float32)
    if split:
        entries = entries * shard_levels(key, dims, split, -0.22, 0.18)
    return jnp.clip(strengthened(entries, jax.random.fold_in(key, 3), *heavy), -bound, bound).astype(kind)


def setup_inputs(seed: int = 0) -> dict:
    keys = jax.random.split(jax.random.key(seed), 14)
    tokens = gaussian_with(keys[0], (TOKENS, D), 1.0, 6.0, ((0, 32),), (0, 1, 32, 2.75))
    w_qkv = noise(keys[1], (D, 3 * D), D ** -0.5, 0.15625, ((0, 32),))
    w_attn_out = noise(keys[2], (D, D), (D // 64) ** -0.5, 1.25, ((0, 32),))
    w_shared_in = noise(keys[3], (D, 2 * SFF), D ** -0.5, 0.15625, ((0, 32),))
    w_shared_out = noise(keys[4], (SFF, D), (SFF // 4) ** -0.5, 0.375, ((0, 32),))
    gain_attn = jnp.clip(1.0 + 0.1 * jax.random.normal(keys[5], (D,), jnp.float32), 0.5, 1.5).astype(jnp.bfloat16)
    gain_ffn = jnp.clip(1.0 + 0.1 * jax.random.normal(keys[6], (D,), jnp.float32), 0.5, 1.5).astype(jnp.bfloat16)
    w_expert_in = noise(keys[7], (EXPERTS, D, 2 * FF), D ** -0.5, 0.15625, ((0, 8),))
    w_expert_out = noise(keys[8], (EXPERTS, FF, D), (FF // 16) ** -0.5, 0.75, ((0, 8),))
    route_ids_keys = jax.random.split(jax.random.fold_in(keys[9], 1), TOKENS // TOK_DEV)
    route_ids_turns = jax.random.permutation(jax.random.fold_in(keys[9], 3), TOKENS // TOK_DEV)
    route_ids = jax.vmap(lambda own, number: shared_out(jax.random.fold_in(keys[9], 2), own, number, TOK_DEV, EXPERTS, TOP, CAP, 1))(route_ids_keys, route_ids_turns).reshape((TOKENS, TOP))
    route_gates = jnp.clip(0.08 + 0.17 * jax.random.uniform(keys[10], (TOKENS, TOP), jnp.float32) ** shard_levels(keys[10], (TOKENS, TOP), ((0, 32),), -0.2, 0.2), 0.08, 0.25)
    seq_lengths = ragged_sizes(keys[11], SEQS, 3 * TOK_DEV * SEQS // 4, TOK_DEV, 2).astype(jnp.int32)
    cotangent = noise(keys[12], (TOKENS, D), 1.0, 6.0, ((0, 32),))
    return dict(tokens=tokens, w_qkv=w_qkv, w_attn_out=w_attn_out, w_shared_in=w_shared_in, w_shared_out=w_shared_out, gain_attn=gain_attn, gain_ffn=gain_ffn, w_expert_in=w_expert_in, w_expert_out=w_expert_out, route_ids=route_ids, route_gates=route_gates, seq_lengths=seq_lengths, cotangent=cotangent)


highest = lax.Precision.HIGHEST
norm_eps = 1e-06

@jax.custom_vjp
def low(v):
    return lax.optimization_barrier(v.astype(jnp.bfloat16)).astype(jnp.float32)

@jax.custom_vjp
def low_back(v):
    return v

def low_keep(v):
    return (low(v), None)

def low_pass(kept, grad):
    return (grad,)

def back_keep(v):
    return (v, None)

def back_low(kept, grad):
    return (low(grad),)
low.defvjp(low_keep, low_pass)
low_back.defvjp(back_keep, back_low)

def matmul_hi(left, right):
    return jnp.dot(left, right, precision=highest)

def rms_norm(activation, norm_gain):
    return activation * lax.rsqrt(lax.optimization_barrier(jnp.mean(activation * activation, axis=-1, keepdims=True)) + norm_eps) * norm_gain

def swish_product(gate_up, hidden_width):
    gate_part = gate_up[..., :hidden_width]
    return gate_part * jax.nn.sigmoid(gate_part) * gate_up[..., hidden_width:]

def rotary_tables(positions, head_dim):
    half_dim = head_dim // 2
    frequencies = 10000.0 ** (-(2.0 * jnp.arange(half_dim, dtype=jnp.float32)) / head_dim)
    angles = positions.astype(jnp.float32)[:, None] * frequencies[None, :]
    return (jnp.cos(angles)[:, None, :], jnp.sin(angles)[:, None, :])

def rotate(head_rows, cosine, sine_table):
    half_dim = head_rows.shape[-1] // 2
    first_half = head_rows[..., :half_dim]
    second = head_rows[..., half_dim:]
    return jnp.concatenate([first_half * cosine - second * sine_table, second * cosine + first_half * sine_table], axis=-1)

def attend_sequence(packed):
    queries, key_rows, value_rows, length = packed
    row_count = queries.shape[0]
    scores = jnp.einsum('qhd,khd->hqk', queries, key_rows, precision=highest) * queries.shape[-1] ** (-0.5)
    scores = low_back(scores)
    positions = jnp.arange(row_count)
    allowed = (positions[None, :] <= positions[:, None]) & (positions[None, :] < length)
    scores = jnp.where(allowed[None], scores, -1e+30)
    row_peak = lax.optimization_barrier(jnp.max(scores, axis=-1, keepdims=True))
    exp_scores = jnp.exp(scores - row_peak)
    attention_weights = low(exp_scores / lax.optimization_barrier(jnp.sum(exp_scores, axis=-1, keepdims=True)))
    return jnp.einsum('hqk,khd->qhd', attention_weights, value_rows, precision=highest)

def reference(tokens, w_qkv, w_attn_out, w_shared_in, w_shared_out, gain_attn, gain_ffn, w_expert_in, w_expert_out, route_ids, route_gates, seq_lengths, cotangent):
    positions = jnp.arange(TOKENS) % TOK_DEV
    sequence_of = jnp.arange(TOKENS) // TOK_DEV
    live_rows = (positions < seq_lengths[sequence_of]).astype(jnp.float32)
    chosen = (route_ids[:, :, None] == jnp.arange(EXPERTS)[None, None, :]).astype(jnp.float32)
    live_gates = route_gates.astype(jnp.float32) * live_rows[:, None]
    weights = lax.optimization_barrier(jnp.sum(chosen * live_gates[:, :, None], axis=1))
    counts = lax.optimization_barrier(jnp.sum(chosen * live_rows[:, None, None], axis=(0, 1))).astype(jnp.int32)
    cosine, sine_table = rotary_tables(positions, HEAD_DIM)

    def forward(tokens_f, qkv_f, attn_out_f, shared_in_f, shared_out_f, gain_one, gain_two, expert_in_f, expert_out_f):
        normed = low(rms_norm(tokens_f, gain_one))
        projected = low_back(matmul_hi(normed, qkv_f))
        head_shape = (TOKENS, HEADS, HEAD_DIM)
        queries = low(rotate(projected[:, :D].reshape(head_shape), cosine, sine_table))
        key_rows = low(rotate(projected[:, D:2 * D].reshape(head_shape), cosine, sine_table))
        value_rows = low(projected[:, 2 * D:].reshape(head_shape))
        seq_shape = (SEQS, TOK_DEV, HEADS, HEAD_DIM)
        attended = lax.map(jax.checkpoint(attend_sequence), (queries.reshape(seq_shape), key_rows.reshape(seq_shape), value_rows.reshape(seq_shape), seq_lengths))
        attended = low_back(low(attended.reshape(TOKENS, D)))
        residual = tokens_f + matmul_hi(attended, attn_out_f)
        normed_ffn = low(rms_norm(residual, gain_two))
        shared_gate_up = low_back(matmul_hi(normed_ffn, shared_in_f))
        shared_hidden = low(swish_product(shared_gate_up, SFF))
        result = residual + matmul_hi(shared_hidden, shared_out_f)

        def expert_step(running, packed):
            weight_in, weight_out, expert_weight = packed
            token_rows = low_back(normed_ffn)
            gate_up = low_back(matmul_hi(token_rows, weight_in))
            hidden = low(swish_product(gate_up, FF))
            output = low_back(low(matmul_hi(hidden, weight_out)))
            return (running + expert_weight[:, None] * output, None)
        routed, unused = lax.scan(jax.checkpoint(expert_step), jnp.zeros((TOKENS, D), jnp.float32), (expert_in_f, expert_out_f, weights.T))
        return result + routed
    output, pullback = jax.vjp(forward, tokens.astype(jnp.float32), w_qkv.astype(jnp.float32), w_attn_out.astype(jnp.float32), w_shared_in.astype(jnp.float32), w_shared_out.astype(jnp.float32), gain_attn.astype(jnp.float32), gain_ffn.astype(jnp.float32), w_expert_in.astype(jnp.float32), w_expert_out.astype(jnp.float32))
    gradients = pullback(cotangent.astype(jnp.float32))
    return (output.astype(jnp.bfloat16), gradients[0], gradients[1], gradients[2], gradients[3], gradients[4], gradients[5], gradients[6], gradients[7], gradients[8], counts)
```

```python
import functools

import jax
import jax.numpy as jnp
from jax import lax
from jax.experimental import pallas as pl
from jax.experimental.pallas import tpu as pltpu
from jax.sharding import PartitionSpec as P

HEADS = 10
HEAD_DIM = 128
TOP = 6
norm_eps = 1e-06

BF = jnp.bfloat16
F32 = jnp.float32
BOTH = ("dp", "expert")


def rotary_tables(positions, head_dim):
    half_dim = head_dim // 2
    frequencies = 10000.0 ** (-(2.0 * jnp.arange(half_dim, dtype=F32)) / head_dim)
    angles = positions.astype(F32)[:, None] * frequencies[None, :]
    return (jnp.cos(angles)[:, None, :], jnp.sin(angles)[:, None, :])


def rotate(head_rows, cosine, sine_table):
    half_dim = head_rows.shape[-1] // 2
    first_half = head_rows[..., :half_dim]
    second = head_rows[..., half_dim:]
    return jnp.concatenate(
        [first_half * cosine - second * sine_table, second * cosine + first_half * sine_table],
        axis=-1,
    )


def unrotate(head_grads, cosine, sine_table):
    return rotate(head_grads, cosine, -sine_table)


def contract_rows(left, right):
    return lax.dot_general(left, right, (((0,), (0,)), ((), ())), preferred_element_type=F32)


def times_transposed(left, right):
    return lax.dot_general(left, right, (((1,), (1,)), ((), ())), preferred_element_type=F32)


def swish_product(gate_up, hidden_width):
    gate_part = gate_up[..., :hidden_width]
    return gate_part * jax.nn.sigmoid(gate_part) * gate_up[..., hidden_width:]


def swish_back(grad_hidden, gate_up, hidden_width):
    gate_part = gate_up[..., :hidden_width]
    up_part = gate_up[..., hidden_width:]
    sigmoid_gate = jax.nn.sigmoid(gate_part)
    grad_gate = grad_hidden * up_part * sigmoid_gate * (1.0 + gate_part * (1.0 - sigmoid_gate))
    grad_up = grad_hidden * gate_part * sigmoid_gate
    return jnp.concatenate([grad_gate, grad_up], axis=-1)


def norm_scale(activation):
    return lax.rsqrt(jnp.mean(activation * activation, axis=-1, keepdims=True) + norm_eps)


def norm_back(grad_normed, activation, row_scale, norm_gain):
    weighted = grad_normed * norm_gain
    grad_input = row_scale * weighted - activation * row_scale**3 * jnp.mean(
        weighted * activation, axis=-1, keepdims=True
    )
    return (grad_input, jnp.sum(grad_normed * activation * row_scale, axis=0))


def dot(left, right, left_dim=1, right_dim=0):
    return lax.dot_general(
        left, right, (((left_dim,), (right_dim,)), ((), ())), preferred_element_type=F32
    )


def expert_body(
    rank_ref, gate_ref, rows_ref, grads_ref, win_ref, wout_ref,
    pdx_ref, pout_ref, x_ref, h_ref, gr_ref, dgu_ref, *, capacity, hidden,
):
    experts = win_ref.shape[0]
    slot = lax.broadcasted_iota(jnp.int32, (capacity, rows_ref.shape[1]), 0)
    rows, grads = rows_ref[0], grads_ref[0]
    picks, back_rows, results = [], [], []
    for e in range(experts):
        mask = slot == rank_ref[0, e : e + 1, :]
        pick = jnp.where(mask, 1.0, 0.0).astype(BF)
        gate_col = jnp.sum(
            jnp.where(mask, gate_ref[0, e : e + 1, :], 0.0), axis=1, keepdims=True
        )
        x = dot(pick, rows).astype(BF)
        x_ref[e, 0] = x
        gate_up = dot(x, win_ref[e])
        a, b = gate_up[:, :hidden], gate_up[:, hidden:]
        s = jax.nn.sigmoid(a)
        swish = a * s
        h = (swish * b).astype(BF)
        h_ref[e, 0] = h
        gr = (dot(pick, grads) * gate_col).astype(BF)
        gr_ref[e, 0] = gr
        gh = dot(gr, wout_ref[e], 1, 1)
        dgu_ref[e, 0, :, :hidden] = (gh * b * s * (1.0 + a * (1.0 - s))).astype(BF)
        dgu_ref[e, 0, :, hidden:] = (gh * swish).astype(BF)
        back_rows.append(dot(dgu_ref[e, 0], win_ref[e], 1, 1).astype(BF))
        results.append((dot(h, wout_ref[e]) * gate_col).astype(BF))
        picks.append(pick)
    picks = jnp.concatenate(picks, axis=0)
    pdx_ref[0] = dot(picks, jnp.concatenate(back_rows, axis=0), 0, 0).astype(BF)
    pout_ref[0] = dot(picks, jnp.concatenate(results, axis=0), 0, 0).astype(BF)


def expert_rows(rank, gate, rows, grads, w_in, w_out, capacity):
    n, row_count, width = rows.shape
    experts, hidden, _ = w_out.shape
    full = lambda shape: pl.BlockSpec(
        shape, lambda i: (0,) * len(shape), pipeline_mode=pl.Buffered(1)
    )
    block = lambda *shape: pl.BlockSpec((1,) + shape, lambda i: (i, 0, 0))
    slots = lambda w: pl.BlockSpec((experts, 1, capacity, w), lambda i: (0, i, 0, 0))
    widths = (width, hidden, width, 2 * hidden)
    return pl.pallas_call(
        functools.partial(expert_body, capacity=capacity, hidden=hidden),
        grid=(n,),
        in_specs=[
            block(experts, row_count),
            block(experts, row_count),
            block(row_count, width),
            block(row_count, width),
            full(w_in.shape),
            full(w_out.shape),
        ],
        out_specs=[block(row_count, width), block(row_count, width)] + [slots(w) for w in widths],
        out_shape=[jax.ShapeDtypeStruct((n, row_count, width), BF)] * 2
        + [jax.ShapeDtypeStruct((experts, n, capacity, w), BF) for w in widths],
        compiler_params=pltpu.CompilerParams(vmem_limit_bytes=60 * 2**20),
        cost_estimate=pl.CostEstimate(
            flops=n * 9_300_000_000, bytes_accessed=n * 8_000_000 + 14_000_000, transcendentals=0
        ),
        name="expert_rows",
    )(rank, gate, rows, grads, w_in, w_out)


def sum_over_dp(array):
    count = lax.axis_size("dp")
    index = lax.axis_index("dp")
    core = index % 2
    swap = [(i, i ^ 1) for i in range(count)]
    first, second = array[0], array[1]
    mine = jnp.where(core == 0, first, second)
    other = jnp.where(core == 0, second, first)
    got = lax.ppermute(other, "dp", swap)
    total = (mine.astype(F32) + got.astype(F32)).astype(BF)
    step = 2
    while step < count:
        got = lax.ppermute(total, "dp", [(i, i ^ step) for i in range(count)])
        total = (total.astype(F32) + got.astype(F32)).astype(BF)
        step *= 2
    got = lax.ppermute(total, "dp", swap)
    return jnp.stack(
        [jnp.where(core == 0, total, got), jnp.where(core == 0, got, total)]
    ).astype(F32)


def on_device(
    tokens, w_qkv, w_attn_out, w_shared_in, w_shared_out, gain_attn, gain_ffn,
    w_expert_in, w_expert_out, route_ids, route_gates, seq_lengths, cotangent,
):
    row_count, model_width = tokens.shape
    groups = lax.axis_size("expert")
    local_experts = w_expert_in.shape[0]
    experts_total = local_experts * groups
    capacity = row_count * TOP * 5 // (4 * experts_total)

    qkv_full = lax.all_gather(w_qkv, BOTH, axis=0, tiled=True)
    out_full = lax.all_gather(w_attn_out, BOTH, axis=0, tiled=True)
    shared_in_full = lax.all_gather(w_shared_in, BOTH, axis=0, tiled=True)
    shared_out_full = lax.all_gather(w_shared_out, BOTH, axis=0, tiled=True)
    gains = lax.all_gather(jnp.stack([gain_attn, gain_ffn]), BOTH, axis=1, tiled=True)
    gain_first, gain_second = gains[0].astype(F32), gains[1].astype(F32)
    shared_width = shared_out_full.shape[0]
    score_scale = HEAD_DIM ** (-0.5)

    positions = jnp.arange(row_count)
    cosine, sine_table = rotary_tables(positions, HEAD_DIM)
    length = seq_lengths[0]
    live_rows = positions < length
    live_ids = jnp.where(live_rows[:, None], route_ids, -1).T
    counts = lax.psum(
        jnp.sum(
            (live_ids[:, :, None] == jnp.arange(experts_total)[None, None, :]).astype(jnp.int32),
            axis=(0, 1),
        ),
        BOTH,
    )
    routes = lax.all_gather(
        jnp.concatenate([live_ids.astype(F32), route_gates.T], axis=0), "expert", axis=0
    )
    mine = (
        lax.axis_index("expert") * local_experts + jnp.arange(local_experts)
    ).astype(F32)
    chosen = routes[:, None, :TOP, :] == mine[None, :, None, None]
    slot_gate = jnp.sum(jnp.where(chosen, routes[:, None, TOP:, :], 0.0), axis=2)
    named = jnp.any(chosen, axis=2)
    earlier = (positions[:, None] < positions[None, :]).astype(BF)
    rank = jnp.dot(
        named.astype(BF).reshape(groups * local_experts, row_count),
        earlier,
        preferred_element_type=F32,
    ).reshape(named.shape)
    slot_rank = jnp.where(named, rank.astype(jnp.int32), -1)
    grads_all = lax.all_gather(cotangent, "expert", axis=0)

    allowed = (positions[None, :] <= positions[:, None]) & (positions[None, :] < length)
    head_shape = (row_count, HEADS, HEAD_DIM)
    tokens_f = tokens.astype(F32)
    scale_first = norm_scale(tokens_f)
    normed_first = (tokens_f * scale_first * gain_first).astype(BF)
    projected = jnp.dot(normed_first, qkv_full, preferred_element_type=F32)
    queries = rotate(projected[:, :model_width].reshape(head_shape), cosine, sine_table).astype(BF)
    key_rows = rotate(
        projected[:, model_width : 2 * model_width].reshape(head_shape), cosine, sine_table
    ).astype(BF)
    value_rows = projected[:, 2 * model_width :].reshape(head_shape).astype(BF)
    scores = (
        jnp.einsum("qhd,khd->hqk", queries, key_rows, preferred_element_type=F32) * score_scale
    )
    scores = jnp.where(allowed[None], scores, -1e30)
    row_peak = jnp.max(scores, axis=-1, keepdims=True)
    exp_scores = jnp.exp(scores - row_peak)
    row_sum = jnp.sum(exp_scores, axis=-1, keepdims=True)
    log_total = row_peak + jnp.log(row_sum)
    attention_weights = (exp_scores / row_sum).astype(BF)
    attended = (
        jnp.einsum("hqk,khd->qhd", attention_weights, value_rows, preferred_element_type=F32)
        .reshape(row_count, model_width)
        .astype(BF)
    )
    residual = tokens_f + jnp.dot(attended, out_full, preferred_element_type=F32)
    scale_second = norm_scale(residual)
    normed_second = (residual * scale_second * gain_second).astype(BF)

    rows_all = lax.all_gather(normed_second, "expert", axis=0)
    part_back, part_out, x, hidden, result_grad, gate_up_grad = expert_rows(
        slot_rank, slot_gate, rows_all, grads_all, w_expert_in, w_expert_out, capacity
    )
    flat = lambda a: a.reshape(groups * row_count, model_width)
    routed_back = lax.psum_scatter(flat(part_back), "expert", scatter_dimension=0, tiled=True)
    routed_out = lax.psum_scatter(flat(part_out), "expert", scatter_dimension=0, tiled=True)
    grad_in = jnp.einsum("esrd,esrf->edf", x, gate_up_grad, preferred_element_type=F32)
    grad_down = jnp.einsum("esrf,esrd->efd", hidden, result_grad, preferred_element_type=F32)
    grad_in = sum_over_dp(grad_in.astype(BF))
    grad_down = sum_over_dp(grad_down.astype(BF))

    gradient = cotangent.astype(F32)
    shared_gate_up = jnp.dot(normed_second, shared_in_full, preferred_element_type=F32)
    shared_hidden = swish_product(shared_gate_up, shared_width).astype(BF)
    layer_sum = residual + jnp.dot(shared_hidden, shared_out_full, preferred_element_type=F32)
    grad_shared_out = contract_rows(shared_hidden, cotangent)
    grad_shared_hidden = times_transposed(cotangent, shared_out_full)
    grad_shared_gate_up = swish_back(grad_shared_hidden, shared_gate_up, shared_width).astype(BF)
    grad_shared_in = contract_rows(normed_second, grad_shared_gate_up)
    block_out = (layer_sum + routed_out.astype(F32)).astype(BF)

    scatter = lambda a: lax.psum_scatter(
        a.astype(BF), BOTH, scatter_dimension=0, tiled=True
    ).astype(F32)
    share_shared_in = scatter(grad_shared_in)
    share_shared_out = scatter(grad_shared_out)

    grad_normed_second = times_transposed(grad_shared_gate_up, shared_in_full) + routed_back.astype(
        F32
    )
    grad_residual_part, grad_gain_second = norm_back(
        grad_normed_second, residual, scale_second, gain_second
    )
    grad_residual = gradient + grad_residual_part
    grad_residual_low = grad_residual.astype(BF)
    share_out = scatter(contract_rows(attended, grad_residual_low))

    grad_attended = times_transposed(grad_residual_low, out_full).astype(BF).reshape(head_shape)
    scores = (
        jnp.einsum("qhd,khd->hqk", queries, key_rows, preferred_element_type=F32) * score_scale
    )
    scores = jnp.where(allowed[None], scores, -1e30)
    attention_probs = jnp.exp(scores - log_total)
    grad_weights = jnp.einsum("qhd,khd->hqk", grad_attended, value_rows, preferred_element_type=F32)
    row_delta = jnp.sum(grad_weights * attention_probs, axis=-1, keepdims=True)
    grad_scores = (attention_probs * (grad_weights - row_delta)).astype(BF)
    grad_values = jnp.einsum(
        "hqk,qhd->khd", attention_probs.astype(BF), grad_attended, preferred_element_type=F32
    )
    grad_queries = unrotate(
        jnp.einsum("hqk,khd->qhd", grad_scores, key_rows, preferred_element_type=F32) * score_scale,
        cosine,
        sine_table,
    )
    grad_keys = unrotate(
        jnp.einsum("hqk,qhd->khd", grad_scores, queries, preferred_element_type=F32) * score_scale,
        cosine,
        sine_table,
    )
    grad_projected = jnp.concatenate(
        [
            grad_queries.reshape(row_count, model_width),
            grad_keys.reshape(row_count, model_width),
            grad_values.reshape(row_count, model_width),
        ],
        axis=1,
    ).astype(BF)
    share_qkv = scatter(contract_rows(normed_first, grad_projected))
    grad_normed_first = times_transposed(grad_projected, qkv_full)
    grad_tokens_part, grad_gain_first = norm_back(
        grad_normed_first, tokens_f, scale_first, gain_first
    )
    grad_tokens = grad_residual + grad_tokens_part
    share_gain = lax.psum_scatter(
        jnp.stack([grad_gain_first, grad_gain_second]), BOTH, scatter_dimension=1, tiled=True
    )
    return (
        block_out, grad_tokens, share_qkv, share_out, share_shared_in, share_shared_out,
        share_gain[0], share_gain[1], grad_in, grad_down, counts,
    )


def solution(mesh):
    rows = P(BOTH, None)
    flat = P(BOTH)
    experts = P("expert", None, None)
    return jax.shard_map(
        on_device,
        mesh=mesh,
        in_specs=(
            rows, rows, rows, rows, rows, flat, flat, experts, experts, rows, rows, flat, rows,
        ),
        out_specs=(
            rows, rows, rows, rows, rows, rows, flat, flat, experts, experts, P(),
        ),
        check_vma=False,
    )
```

```python
import functools

import jax
import jax.numpy as jnp
from jax import lax
from jax.experimental import pallas as pl
from jax.experimental.pallas import tpu as pltpu
from jax.sharding import PartitionSpec as P

HEADS = 10
HEAD_DIM = 128
TOP = 6
PAIR = 2 * HEAD_DIM
ROUTE_ROWS = 16
norm_eps = 1e-06

BF = jnp.bfloat16
F32 = jnp.float32
BOTH = ("dp", "expert")
together = lax.optimization_barrier


def dot(left, right, left_dim=1, right_dim=0):
    return lax.dot_general(
        left, right, (((left_dim,), (right_dim,)), ((), ())), preferred_element_type=F32
    )


def add(left, right):
    return (left.astype(F32) + right.astype(F32)).astype(BF)


def norm_scale(activation):
    return lax.rsqrt(jnp.mean(activation * activation, axis=-1, keepdims=True) + norm_eps)


def full_block(*shape):
    return pl.BlockSpec(
        shape, lambda *i: (0,) * len(shape), pipeline_mode=pl.Buffered(1)
    )


def shaped(*shape, dtype=BF):
    return jax.ShapeDtypeStruct(shape, dtype)


def kernel_cost(flops, moved):
    return pl.CostEstimate(flops=flops, bytes_accessed=moved, transcendentals=0)


def rotary_tables(row_count):
    half = HEAD_DIM // 2
    frequencies = 10000.0 ** (-(2.0 * jnp.arange(half, dtype=F32)) / HEAD_DIM)
    angles = jnp.arange(row_count).astype(F32)[:, None] * frequencies[None, :]
    cosine, sine = jnp.cos(angles), jnp.sin(angles)
    return (
        jnp.concatenate([cosine, cosine], axis=1),
        jnp.concatenate([-sine, sine], axis=1),
    )


def turn(head, cosine, sine):
    return head * cosine + pltpu.roll(head, HEAD_DIM // 2, 1) * sine


def turn_back(head, cosine, sine):
    return head * cosine - pltpu.roll(head, HEAD_DIM // 2, 1) * sine


def allowed_keys(start, stop, length):
    shape = (stop - start, stop)
    row = lax.broadcasted_iota(jnp.int32, shape, 0) + start
    column = lax.broadcasted_iota(jnp.int32, shape, 1)
    return (column <= row) & (column < length)


def attend_body(
    length_ref, wq_ref, wk_ref, wv_ref, wo_ref, gains_in_ref, cos_ref, sin_ref, tokens_ref,
    q_ref, k_ref, v_ref, att_ref, lse_ref, normed_ref, gains_ref, residual_ref, normed_second_ref,
    total_ref,
):
    step = pl.program_id(0)
    row_count = tokens_ref.shape[0]

    @pl.when(step == 0)
    def _():
        shape = (gains_ref.shape[0], HEAD_DIM)
        pick = lax.broadcasted_iota(jnp.int32, shape, 0) == lax.broadcasted_iota(
            jnp.int32, shape, 1
        )
        gains = dot(jnp.where(pick, 1.0, 0.0).astype(BF), gains_in_ref[...], 1, 1)
        gains_ref[...] = gains
        value = tokens_ref[...].astype(F32)
        normed_ref[...] = (value * norm_scale(value) * gains[0:1]).astype(BF)
        total_ref[...] = value

    normed = normed_ref[...]
    length = length_ref[0]
    cosine, sine = cos_ref[...], sin_ref[...]
    queries, keys = dot(normed, wq_ref[...]), dot(normed, wk_ref[...])
    v_ref[...] = dot(normed, wv_ref[...]).astype(BF)
    for head in range(2):
        here = slice(head * HEAD_DIM, (head + 1) * HEAD_DIM)
        q = turn(queries[:, here], cosine, sine).astype(BF)
        k = turn(keys[:, here], cosine, sine).astype(BF)
        q_ref[:, here] = q
        k_ref[:, here] = k
        for start in range(0, row_count, row_count // 2):
            stop = start + row_count // 2
            scores = dot(q[start:stop], k[:stop], 1, 1) * HEAD_DIM ** (-0.5)
            scores = jnp.where(allowed_keys(start, stop, length), scores, -1e30)
            peak = jnp.max(scores, axis=1, keepdims=True)
            weights = jnp.exp(scores - peak)
            whole = jnp.sum(weights, axis=1, keepdims=True)
            lse_ref[0, start:stop, head : head + 1] = peak + jnp.log(whole)
            att_ref[start:stop, here] = dot(
                (weights * (1.0 / whole)).astype(BF), v_ref[:stop, here]
            ).astype(BF)

    total_ref[...] += dot(att_ref[...], wo_ref[...])

    @pl.when(step == pl.num_programs(0) - 1)
    def _():
        residual = total_ref[...]
        residual_ref[...] = residual
        normed_second_ref[...] = (residual * norm_scale(residual) * gains_ref[1:2]).astype(BF)


def attend(length, weights, cosine, sine, tokens):
    rows, width = tokens.shape
    steps = width // PAIR
    part = lambda offset: pl.BlockSpec((width, PAIR), lambda i: (0, i + offset))
    pair = pl.BlockSpec((rows, PAIR), lambda i: (0, i))
    whole = full_block(rows, width)
    return pl.pallas_call(
        attend_body,
        grid=(steps,),
        in_specs=[
            pl.BlockSpec(memory_space=pltpu.SMEM),
            part(0),
            part(steps),
            part(2 * steps),
            pl.BlockSpec((PAIR, width), lambda i: (i, 3)),
            pl.BlockSpec((width, HEAD_DIM), lambda i: (0, 4 * HEADS), pipeline_mode=pl.Buffered(1)),
            full_block(rows, HEAD_DIM),
            full_block(rows, HEAD_DIM),
            whole,
        ],
        out_specs=[pair] * 4
        + [
            pl.BlockSpec((1, rows, 2), lambda i: (i, 0, 0)),
            whole,
            full_block(8, width),
            whole,
            whole,
        ],
        out_shape=[shaped(rows, width)] * 4
        + [
            shaped(steps, rows, 2, dtype=F32), shaped(rows, width), shaped(8, width, dtype=F32),
            shaped(rows, width, dtype=F32), shaped(rows, width),
        ],
        scratch_shapes=[pltpu.VMEM((rows, width), F32)],
        compiler_params=pltpu.CompilerParams(vmem_limit_bytes=48 * 2**20),
        cost_estimate=kernel_cost(10_000_000_000, 25_000_000),
        name="attend",
    )(length, weights, weights, weights, weights, weights, cosine, sine, tokens)


def middle_body(
    pre_ref, own_ref, one_ref, two_ref, residual_ref, cot_ref, gain_ref, wo_ref,
    gr_ref, grb_ref, datt_ref, prod_ref,
):
    @pl.when(pl.program_id(0) == 0)
    def _():
        value = residual_ref[...]
        scale = norm_scale(value)
        grad = pre_ref[...] + (
            own_ref[...].astype(F32) + one_ref[...].astype(F32) + two_ref[...].astype(F32)
        )
        weighted = grad * gain_ref[1:2]
        out = cot_ref[...].astype(F32) + (
            scale * weighted
            - value * (scale * scale * scale) * jnp.mean(weighted * value, axis=1, keepdims=True)
        )
        gr_ref[...] = out
        grb_ref[...] = out.astype(BF)
        prod_ref[...] = (grad * value * scale).astype(BF)

    datt_ref[...] = dot(grb_ref[...], wo_ref[...], 1, 1).astype(BF)


def middle(pre, own, one, two, residual, cot, gain, weights):
    rows, width = residual.shape
    steps = width // PAIR
    pair = pl.BlockSpec((rows, PAIR), lambda i: (0, i))
    whole = full_block(rows, width)
    return pl.pallas_call(
        middle_body,
        grid=(steps,),
        in_specs=[whole] * 6
        + [full_block(8, width), pl.BlockSpec((PAIR, width), lambda i: (i, 3))],
        out_specs=[whole, whole, pair, whole],
        out_shape=[
            shaped(rows, width, dtype=F32), shaped(rows, width), shaped(rows, width),
            shaped(rows, width),
        ],
        compiler_params=pltpu.CompilerParams(vmem_limit_bytes=48 * 2**20),
        cost_estimate=kernel_cost(4_000_000_000, 25_000_000),
        name="middle",
    )(pre, own, one, two, residual, cot, gain, weights)


def attend_back_body(
    length_ref, normed_ref, wq_ref, wk_ref, wv_ref, cos_ref, sin_ref, tokens_ref, gain_ref,
    q_ref, k_ref, v_ref, datt_ref, lse_ref, gr_ref, grb_ref, att_ref, prod_ref,
    mine_ref, other_ref, gtok_ref, mine_late_ref, other_late_ref,
    gq_ref, gk_ref, gv_ref, total_ref, *, chips,
):
    step = pl.program_id(0)
    normed = normed_ref[...]
    row_count, width = normed.shape
    length, core = length_ref[0], length_ref[1]
    cosine, sine = cos_ref[...], sin_ref[...]
    scale = HEAD_DIM ** (-0.5)
    unit = width // (2 * chips)

    def store(refs, columns, block):
        block = block.astype(BF)
        for mine in range(2):

            @pl.when(core == mine)
            def _(mine=mine):
                for n in range(2 * chips):
                    ref = refs[0] if n % 2 == mine else refs[1]
                    ref[n // 2 * unit : (n // 2 + 1) * unit, columns] = block[
                        n * unit : (n + 1) * unit
                    ]

    half = row_count // 2
    for head in range(2):
        here = slice(head * HEAD_DIM, (head + 1) * HEAD_DIM)
        grad_keys, grad_values = [], []
        for start in (0, half):
            stop = start + half
            q, k = q_ref[start:stop, here], k_ref[:stop, here]
            grad = datt_ref[start:stop, here]
            scores = dot(q, k, 1, 1) * scale
            scores = jnp.where(allowed_keys(start, stop, length), scores, -1e30)
            probs = jnp.exp(scores - lse_ref[0, start:stop, head : head + 1])
            grad_probs = dot(grad, v_ref[:stop, here], 1, 1)
            delta = jnp.sum(grad_probs * probs, axis=1, keepdims=True)
            grad_scores = (probs * (grad_probs - delta)).astype(BF)
            grad_values.append(dot(probs.astype(BF), grad, 0, 0))
            gq_ref[start:stop, here] = turn_back(
                dot(grad_scores, k) * scale, cosine[start:stop], sine[start:stop]
            ).astype(BF)
            grad_keys.append(dot(grad_scores, q, 0, 0) * scale)
        for out_ref, (first, second), turned in (
            (gk_ref, grad_keys, True),
            (gv_ref, grad_values, False),
        ):
            whole = jnp.concatenate([first + second[:half], second[half:]], axis=0)
            if turned:
                whole = turn_back(whole, cosine, sine)
            out_ref[:, here] = whole.astype(BF)

    @pl.when(step == 0)
    def _():
        total_ref[...] = jnp.zeros_like(total_ref)

    offset = pl.multiple_of(step * 3 * PAIR, PAIR)
    refs = (mine_ref, other_ref)
    for n, (grad_ref, w_ref) in enumerate(((gq_ref, wq_ref), (gk_ref, wk_ref), (gv_ref, wv_ref))):
        grad = grad_ref[...]
        store(refs, pl.ds(offset + n * PAIR, PAIR), dot(normed, grad, 0, 0))
        total_ref[...] += dot(grad, w_ref[...], 1, 1)

    @pl.when(step == pl.num_programs(0) - 1)
    def _():
        value = tokens_ref[...].astype(F32)
        r = norm_scale(value)
        grad = total_ref[...]
        weighted = grad * gain_ref[0:1]
        gtok_ref[...] = gr_ref[...] + (
            r * weighted
            - value * (r * r * r) * jnp.mean(weighted * value, axis=1, keepdims=True)
        )
        lane = lax.broadcasted_iota(jnp.int32, (row_count, HEAD_DIM), 1)
        first = jnp.where(lane == 0, 1.0, 0.0).astype(BF)
        second = jnp.where(lane == 1, 1.0, 0.0).astype(BF)
        refs = (mine_late_ref, other_late_ref)
        store(
            refs,
            slice(width, width + HEAD_DIM),
            dot((grad * value * r).astype(BF), first, 0, 0) + dot(prod_ref[...], second, 0, 0),
        )
        store(refs, slice(0, width), dot(att_ref[...], grb_ref[...], 0, 0))


def attend_back(
    length, normed, weights, cosine, sine, tokens, gain, q, k, v, datt, lse, gr, grb, att, prod, chips
):
    rows, width = tokens.shape
    steps = width // PAIR
    part = lambda offset: pl.BlockSpec((width, PAIR), lambda i: (0, i + offset))
    pair = pl.BlockSpec((rows, PAIR), lambda i: (0, i))
    whole = full_block(rows, width)
    return pl.pallas_call(
        functools.partial(attend_back_body, chips=chips),
        grid=(steps,),
        in_specs=[
            pl.BlockSpec(memory_space=pltpu.SMEM),
            whole,
            part(0),
            part(steps),
            part(2 * steps),
            full_block(rows, HEAD_DIM),
            full_block(rows, HEAD_DIM),
            whole,
            full_block(8, width),
            pair, pair, pair, pair,
            pl.BlockSpec((1, rows, 2), lambda i: (i, 0, 0)),
            whole, whole, whole, whole,
        ],
        out_specs=[full_block(width // 2, 3 * width)] * 2
        + [whole]
        + [full_block(width // 2, width + HEAD_DIM)] * 2,
        out_shape=[shaped(width // 2, 3 * width)] * 2
        + [shaped(rows, width, dtype=F32)]
        + [shaped(width // 2, width + HEAD_DIM)] * 2,
        scratch_shapes=[pltpu.VMEM((rows, PAIR), BF)] * 3 + [pltpu.VMEM((rows, width), F32)],
        compiler_params=pltpu.CompilerParams(vmem_limit_bytes=56 * 2**20),
        cost_estimate=kernel_cost(14_000_000_000, 40_000_000),
        name="attend_back",
    )(
        length, normed, weights, weights, weights, cosine, sine, tokens, gain,
        q, k, v, datt, lse, gr, grb, att, prod,
    )


def expert_body(mine_ref, *refs, count, capacity, hidden):
    rows_refs, grads_refs, route_refs = [refs[n * count : (n + 1) * count] for n in range(3)]
    win_hbm, wout_hbm = refs[3 * count : 3 * count + 2]
    win_ref, wout_ref, sems = refs[-3:]
    refs = refs[:-3]
    pdx_refs, pout_refs = refs[-2 * count - 4 : -count - 4], refs[-count - 4 : -4]
    x_ref, h_ref, gr_ref, dgu_ref = refs[-4:]
    step = pl.program_id(0)
    experts = win_ref.shape[0]
    copies = [
        [
            pltpu.make_async_copy(hbm.at[e], ref.at[e], sems.at[e, n])
            for n, (hbm, ref) in enumerate(((win_hbm, win_ref), (wout_hbm, wout_ref)))
        ]
        for e in range(experts)
    ]

    @pl.when(step == 0)
    def _():
        for copy in sum(copies, []):
            copy.start()

    def arrived(copy):
        @pl.when(step == 0)
        def _():
            copy.wait()

    rows, grads, routes = [g[0][...] for g in (rows_refs, grads_refs, route_refs)]
    for n in range(1, count):
        rows = jnp.where(step == n, rows_refs[n][...], rows)
        grads = jnp.where(step == n, grads_refs[n][...], grads)
        routes = jnp.where(step == n, route_refs[n][...], routes)
    row_count = rows.shape[0]
    routes = routes.astype(F32)
    ids = routes[:TOP, :row_count]
    gates = (
        routes[:TOP, row_count : 2 * row_count]
        + routes[TOP : 2 * TOP, :row_count]
        + routes[TOP : 2 * TOP, row_count : 2 * row_count]
    )
    square = (row_count, row_count)
    earlier = lax.broadcasted_iota(jnp.int32, square, 0) < lax.broadcasted_iota(
        jnp.int32, square, 1
    )
    earlier = jnp.where(earlier, 1.0, 0.0).astype(BF)
    slot = lax.broadcasted_iota(jnp.int32, (capacity, row_count), 0)
    picks, back_rows, results = [], [], []
    for e in range(experts):
        chosen = ids == (mine_ref[0] + e).astype(F32)
        named = jnp.sum(jnp.where(chosen, 1.0, 0.0), axis=0, keepdims=True)
        gate = jnp.sum(jnp.where(chosen, gates, 0.0), axis=0, keepdims=True)
        rank = dot(jnp.broadcast_to(named, (16, row_count)).astype(BF), earlier)[0:1]
        mask = slot == jnp.where(named > 0.5, rank, -1.0).astype(jnp.int32)
        pick = jnp.where(mask, 1.0, 0.0).astype(BF)
        gate_col = jnp.sum(jnp.where(mask, gate, 0.0), axis=1, keepdims=True)
        x = dot(pick, rows).astype(BF)
        x_ref[e, 0] = x
        gr = (dot(pick, grads) * gate_col).astype(BF)
        gr_ref[e, 0] = gr
        arrived(copies[e][0])
        gate_up = dot(x, win_ref[e])
        a, b = gate_up[:, :hidden], gate_up[:, hidden:]
        s = jax.nn.sigmoid(a)
        swish = a * s
        h = (swish * b).astype(BF)
        h_ref[e, 0] = h
        arrived(copies[e][1])
        gh = dot(gr, wout_ref[e], 1, 1)
        dgu_ref[e, 0, :, :hidden] = (gh * b * s * (1.0 + a * (1.0 - s))).astype(BF)
        dgu_ref[e, 0, :, hidden:] = (gh * swish).astype(BF)
        back_rows.append(dot(dgu_ref[e, 0], win_ref[e], 1, 1).astype(BF))
        results.append((dot(h, wout_ref[e]) * gate_col).astype(BF))
        picks.append(pick)
    picks = jnp.concatenate(picks, axis=0)
    back = dot(picks, jnp.concatenate(back_rows, axis=0), 0, 0).astype(BF)
    out = dot(picks, jnp.concatenate(results, axis=0), 0, 0).astype(BF)
    for n in range(count):

        @pl.when(step == n)
        def _(n=n):
            pdx_refs[n][...] = back
            pout_refs[n][...] = out


def expert_rows(first, mine, groups, rows, grads, w_in, w_out, capacity, so_far):
    count = len(rows)
    row_count, width = rows[0].shape
    experts, hidden, _ = w_out.shape
    whole = full_block(row_count, width)
    routes = pl.BlockSpec(
        (ROUTE_ROWS, width),
        lambda i, mine: (row_count // ROUTE_ROWS, 0),
        pipeline_mode=pl.Buffered(1),
    )
    slots = lambda w: pl.BlockSpec((experts, 1, capacity, w), lambda i, mine: (0, first + i, 0, 0))
    widths = (width, hidden, width, 2 * hidden)
    so_far = [] if so_far is None else list(so_far)
    out = pl.pallas_call(
        functools.partial(expert_body, count=count, capacity=capacity, hidden=hidden),
        grid_spec=pltpu.PrefetchScalarGridSpec(
            num_scalar_prefetch=1,
            grid=(count,),
            in_specs=[whole] * (2 * count)
            + [routes] * count
            + [pl.BlockSpec(memory_space=pl.ANY)] * (2 + len(so_far)),
            out_specs=[whole] * (2 * count)
            + [slots(w) for w in widths],
            scratch_shapes=[
                pltpu.VMEM(w_in.shape, BF),
                pltpu.VMEM(w_out.shape, BF),
                pltpu.SemaphoreType.DMA((experts, 2)),
            ],
        ),
        out_shape=[shaped(row_count, width)] * (2 * count)
        + [shaped(experts, groups, capacity, w) for w in widths],
        input_output_aliases={3 + 3 * count + n: 2 * count + n for n in range(len(so_far))},
        compiler_params=pltpu.CompilerParams(vmem_limit_bytes=60 * 2**20),
        cost_estimate=kernel_cost(count * 9_300_000_000, count * 8_000_000 + 14_000_000),
        name="expert_rows",
    )(mine, *rows, *grads, *grads, w_in, w_out, *so_far)
    return list(out[:count]), list(out[count : 2 * count]), list(out[2 * count :])


def expert_grads_body(core_ref, left_ref, right_ref, mine_ref, other_ref):
    merge = lambda ref: ref[0].reshape(-1, ref.shape[-1])
    grads = dot(merge(left_ref), merge(right_ref), 0, 0).astype(BF)

    @pl.when(pl.program_id(0) == 0)
    def _():
        mine_ref[...] = grads

    @pl.when(pl.program_id(0) == 1)
    def _():
        other_ref[...] = grads


def expert_grads(core, left, right, columns):
    experts, groups, capacity, width = left.shape
    steps = right.shape[3] // columns
    take = lambda w, pick: pl.BlockSpec((1, groups, capacity, w), pick)
    block = lambda pick: pl.BlockSpec((width, columns), pick)
    return pl.pallas_call(
        expert_grads_body,
        grid_spec=pltpu.PrefetchScalarGridSpec(
            num_scalar_prefetch=1,
            grid=(experts, steps),
            in_specs=[
                take(width, lambda e, i, core: ((e + core[0]) % 2, 0, 0, 0)),
                take(columns, lambda e, i, core: ((e + core[0]) % 2, 0, 0, i)),
            ],
            out_specs=[
                block(lambda e, i, core: (0, jnp.where(e == 0, i, steps - 1))),
                block(lambda e, i, core: (0, jnp.where(e == 0, 0, i))),
            ],
        ),
        out_shape=[shaped(width, right.shape[3])] * 2,
        compiler_params=pltpu.CompilerParams(vmem_limit_bytes=60 * 2**20),
        cost_estimate=kernel_cost(
            2 * experts * groups * capacity * width * right.shape[3], 40_000_000
        ),
        name="expert_grads",
    )(core, left, right)


def both_experts_body(core_ref, mine_ref, other_ref, out_ref):
    out_ref[core_ref[0]] = mine_ref[...].astype(F32)
    out_ref[1 - core_ref[0]] = other_ref[...].astype(F32)


def both_experts(core, mine, other):
    rows, width = mine.shape
    step = rows // 7 if rows % 112 == 0 else rows // 8
    block = pl.BlockSpec((step, width), lambda i, core: (i, 0))
    return pl.pallas_call(
        both_experts_body,
        grid_spec=pltpu.PrefetchScalarGridSpec(
            num_scalar_prefetch=1,
            grid=(rows // step,),
            in_specs=[block, block],
            out_specs=pl.BlockSpec((2, step, width), lambda i, core: (0, i, 0)),
        ),
        out_shape=shaped(2, rows, width, dtype=F32),
        cost_estimate=kernel_cost(rows * width, 12 * rows * width),
        name="both_experts",
    )(core, mine, other)


def shared_body(
    normed_ref, cot_ref, residual_ref, win_ref, wout_ref,
    pre_ref, sum_ref, gin_ref, gout_ref, grad_ref, *, hidden,
):
    normed, cot = normed_ref[...], cot_ref[...]
    gate_up = dot(normed, win_ref[...])
    a, b = gate_up[:, :hidden], gate_up[:, hidden:]
    s = jax.nn.sigmoid(a)
    swish = a * s
    h = (swish * b).astype(BF)
    gh = dot(cot, wout_ref[...], 1, 1)
    grad_ref[:, :hidden] = (gh * b * s * (1.0 + a * (1.0 - s))).astype(BF)
    grad_ref[:, hidden:] = (gh * swish).astype(BF)
    pre_ref[...] = dot(grad_ref[...], win_ref[...], 1, 1)
    sum_ref[...] = residual_ref[...] + dot(h, wout_ref[...])
    gin_ref[...] = dot(normed, grad_ref[...], 0, 0).astype(BF)
    gout_ref[...] = dot(h, cot, 0, 0).astype(BF)


def shared_expert(normed, cot, residual, w_in, w_out):
    rows, width = normed.shape
    hidden = w_out.shape[0]
    whole = full_block(rows, width)
    return pl.pallas_call(
        functools.partial(shared_body, hidden=hidden),
        grid=(1,),
        in_specs=[
            whole, whole, whole, full_block(width, 2 * hidden), full_block(hidden, width),
        ],
        out_specs=[whole, whole, full_block(width, 2 * hidden), full_block(hidden, width)],
        out_shape=[
            shaped(rows, width, dtype=F32), shaped(rows, width, dtype=F32),
            shaped(width, 2 * hidden), shaped(hidden, width),
        ],
        scratch_shapes=[pltpu.VMEM((rows, 2 * hidden), BF)],
        compiler_params=pltpu.CompilerParams(vmem_limit_bytes=56 * 2**20),
        cost_estimate=kernel_cost(14_000_000_000, 25_000_000),
        name="shared_expert",
    )(normed, cot, residual, w_in, w_out)


LINE = 4


def across(array):
    return lax.ppermute(array, "expert", [(i, i ^ 1) for i in range(2 * LINE)])


def along(array, hops):
    return lax.ppermute(
        array, "expert", [(2 * a + side, 2 * b + side) for a, b in hops for side in (0, 1)]
    )


def by_place(place, options):
    result = options[-1]
    for n in range(len(options) - 2, -1, -1):
        result = jnp.where(place == n, options[n], result)
    return result


class Flow:
    def __init__(self, steps):
        self.steps, self.result = steps, None
        self.waiting = next(steps)

    def feed(self, arrived):
        try:
            self.waiting = self.steps.send(arrived)
        except StopIteration as stop:
            self.waiting, self.result = (), stop.value


def advance(flows, done=()):
    arrived, done = together((tuple(f.waiting for f in flows), done))
    for flow, block in zip(flows, arrived):
        flow.feed(block)
    return done


def finish(flow):
    while flow.result is None:
        advance([flow])
    return flow.result


def gather_steps(own, place, slots):
    slots.append(own)
    y0, d1, u1 = yield (
        across(own),
        along(own, [(1, 0), (2, 1), (3, 2)]),
        along(own, [(0, 1), (1, 2), (2, 3)]),
    )
    s1 = jnp.where(place <= 1, d1, u1)
    slots += [y0, s1]
    y1, d2, u2 = yield (
        across(s1),
        along(d1, [(1, 0), (2, 1)]),
        along(u1, [(1, 2), (2, 3)]),
    )
    s2 = by_place(place, [d2, u1, d1, u2])
    slots += [y1, s2]
    y2, ud3 = yield (across(s2), along(jnp.where(place == 2, u2, d2), [(2, 3), (1, 0)]))
    s3 = by_place(place, [ud3, d2, u2, ud3])
    slots += [y2, s3]
    (y3,) = yield (across(s3),)
    slots.append(y3)
    return slots


def reduce_steps(place, parts):
    own, y0, s1, y1, s2, y2, s3, y3 = parts
    (r3,) = yield (across(y3),)
    s3 = add(s3, r3)
    r2, t3 = yield (across(y2), along(s3, [(0, 1), (3, 2)]))
    s2, s3 = add(s2, r2), add(s3, t3)
    r1, up, down = yield (
        across(y1),
        along(jnp.where(place == 0, s2, s3), [(0, 1), (1, 2)]),
        along(jnp.where(place == 3, s2, s3), [(3, 2), (2, 1)]),
    )
    s1 = add(s1, r1)
    m1 = add(s1, jnp.where(place == 1, up, down))
    m2 = add(s2, jnp.where(place == 1, down, up))
    r0, up, down = yield (
        across(y0),
        along(by_place(place, [s1, m1, m2]), [(0, 1), (1, 2), (2, 3)]),
        along(by_place(place, [m2, m2, m1, s1]), [(3, 2), (2, 1), (1, 0)]),
    )
    return add(own, r0), up, down


def pick_half(array, bit, dim):
    return lax.dynamic_index_in_dim(array, bit, dim, keepdims=False)


def split_core(count):
    return [(i, i ^ 1) for i in range(count)]


def home_steps(mine, other, split=True):
    count = lax.axis_size("dp")
    chip = lax.axis_index("dp") // 2
    place, side = lax.axis_index("expert") // 2, lax.axis_index("expert") % 2
    columns = mine.shape[-1]
    (got,) = yield (lax.ppermute(other, "dp", split_core(count)),)
    total = add(mine, got)

    def over_side(part):
        (got,) = yield (across(pick_half(part, 1 - side, 2)),)
        return add(pick_half(part, side, 2), got)

    def over_chips(part):
        while part.shape[0] > 1:
            half = part.shape[0] // 2
            bit = chip // half % 2
            part = part.reshape((2, half) + part.shape[1:])
            (got,) = yield (
                lax.ppermute(
                    pick_half(part, 1 - bit, 0), "dp", [(i, i ^ (2 * half)) for i in range(count)]
                ),
            )
            part = add(pick_half(part, bit, 0), got)
        return part

    if not split:
        part = yield from over_chips(total)
        part = part[0]
        arrived = yield tuple(
            along(
                pick_half(part, (place + hop) % LINE, 0),
                [(n, (n + hop) % LINE) for n in range(LINE)],
            )
            for hop in range(1, LINE)
        )
        part = pick_half(part, place, 0).astype(F32)
        for block in arrived:
            part = part + block.astype(F32)
        (got,) = yield (across(pick_half(part, 1 - side, 0).astype(BF)),)
        return pick_half(part, side, 0) + got.astype(F32)

    cut = columns // 256 * 128
    parts = [total[..., :cut], total[..., cut:]]
    for kinds in ((over_side, over_chips), (over_chips, over_side)):
        flows = [Flow(kind(part)) for kind, part in zip(kinds, parts)]
        while any(f.result is None for f in flows):
            open_flows = [f for f in flows if f.result is None]
            arrived = yield tuple(f.waiting for f in open_flows)
            for flow, block in zip(open_flows, arrived):
                flow.feed(block)
        parts = [f.result for f in flows]
    part = jnp.concatenate([p[0] for p in parts], axis=-1)
    result = pick_half(part, place, 0).astype(F32)
    arrived = yield tuple(
        along(
            pick_half(part, (place + hop) % LINE, 0), [(n, (n + hop) % LINE) for n in range(LINE)]
        )
        for hop in range(1, LINE)
    )
    for block in arrived:
        result = result + block.astype(F32)
    return result


def dp_sum_steps(mine, other, core, pieces):
    count = lax.axis_size("dp")
    (got,) = yield (lax.ppermute(other, "dp", split_core(count)),)
    unit = mine.shape[0] // pieces
    done = []
    for n in range(pieces):
        piece = add(mine[n * unit : (n + 1) * unit], got[n * unit : (n + 1) * unit])
        step = 2
        while step < count:
            (there,) = yield (lax.ppermute(piece, "dp", [(i, i ^ step) for i in range(count)]),)
            piece = add(piece, there)
            step *= 2
        done.append(piece)
    total = jnp.concatenate(done, axis=0)
    (got,) = yield (lax.ppermute(total, "dp", split_core(count)),)
    return both_experts(core, total, got)


def on_device(
    tokens, w_qkv, w_attn_out, w_shared_in, w_shared_out, gain_attn, gain_ffn,
    w_expert_in, w_expert_out, route_ids, route_gates, seq_lengths, cotangent,
):
    rows, width = tokens.shape
    groups = lax.axis_size("expert")
    devices = groups * lax.axis_size("dp")
    experts = w_expert_in.shape[0]
    experts_total = experts * groups
    capacity = rows * TOP * 5 // (4 * experts_total)
    share, share_out = w_qkv.shape[0], w_shared_out.shape[0]
    shared_width = share_out * devices
    place, side = lax.axis_index("expert") // 2, lax.axis_index("expert") % 2

    gain_columns = jnp.pad(
        jnp.stack([gain_attn, gain_ffn], axis=1), ((0, 0), (0, HEAD_DIM - 2))
    )
    attn_full = lax.all_gather(
        jnp.concatenate([w_qkv, w_attn_out, gain_columns], axis=1), BOTH, axis=0, tiled=True
    )
    live = jnp.arange(rows) < seq_lengths[0]
    ids = jnp.where(live[:, None], route_ids, -1).astype(F32).T
    high = lax.reduce_precision(route_gates.T, 8, 7)
    middle_bits = lax.reduce_precision(route_gates.T - high, 8, 7)
    low = route_gates.T - high - middle_bits
    routes = jnp.concatenate(
        [jnp.concatenate([ids, high], axis=1), jnp.concatenate([middle_bits, low], axis=1)], axis=0
    )
    routes = jnp.pad(
        routes, ((0, ROUTE_ROWS - 2 * TOP), (0, width - 2 * rows))
    ).astype(BF)
    grads = []
    grads_flow = Flow(
        gather_steps(jnp.concatenate([cotangent, routes], axis=0), place, grads)
    )
    mine = lax.axis_index("expert")[None] * experts
    cosine, sine = rotary_tables(rows)
    advance([grads_flow])
    attn_full, w_shared_in, w_shared_out = together((attn_full, w_shared_in, w_shared_out))
    shared_full = lax.all_gather(
        jnp.concatenate(
            [w_shared_in, jnp.pad(w_shared_out, ((0, share - share_out), (0, 0)))], axis=1
        ),
        BOTH,
        axis=0,
        tiled=True,
    )
    advance([grads_flow])

    q, k, v, att, lse, normed_first, gains, residual, normed_second = advance(
        [grads_flow], attend(seq_lengths, attn_full, cosine, sine, tokens)
    )

    arrived, back, out, kept = [], [], [], [None]
    rows_flow = Flow(gather_steps(normed_second, place, arrived))

    def through():
        first = len(back)
        new_back, new_out, kept[0] = expert_rows(
            first, mine, groups, arrived[first:], grads[first : len(arrived)],
            w_expert_in, w_expert_out, capacity, kept[0],
        )
        back.extend(new_back)
        out.extend(new_out)

    through()
    while rows_flow.result is None:
        more = [f for f in (grads_flow,) if f.result is None]
        back[:], out[:], kept[0] = advance([rows_flow] + more, (back, out, kept[0]))
        through()
    x, hidden, result_grad, gate_up_grad = kept[0]

    back_flow = Flow(reduce_steps(place, back))
    core = lax.axis_index("dp")[None] % 2
    grad_in = expert_grads(core, x, gate_up_grad, shared_width)
    grad_down = expert_grads(core, hidden, result_grad, width)
    grad_in, grad_down, out, shared_full = advance(
        [back_flow], (grad_in, grad_down, out, shared_full)
    )

    out_flow = Flow(reduce_steps(place, out))
    in_flow = Flow(dp_sum_steps(*grad_in, core, 4))
    down_flow = Flow(dp_sum_steps(*grad_down, core, 2))
    pre, layer_sum, grad_shared_in, grad_shared_out = shared_expert(
        normed_second,
        cotangent,
        residual,
        shared_full,
        shared_full[:, 2 * shared_width :]
        .reshape(devices, share, width)[:, :share_out]
        .reshape(shared_width, width),
    )
    pre, layer_sum, grad_shared_in, grad_shared_out = advance(
        [back_flow, in_flow, down_flow], (pre, layer_sum, grad_shared_in, grad_shared_out)
    )

    def of_core(which):
        part = lambda array: pick_half(
            array.reshape(devices // groups // 2, 2, LINE, 2, -1, array.shape[1]), which, 1
        )
        below = ((0, 0),) * 3 + ((0, share - share_out), (0, 0))
        return jnp.concatenate(
            [part(grad_shared_in), jnp.pad(part(grad_shared_out), below)], axis=-1
        )

    shared_flow = Flow(home_steps(of_core(core[0]), of_core(1 - core[0]), split=False))
    advance([back_flow, out_flow, in_flow, down_flow])
    advance([back_flow, out_flow, in_flow, down_flow, shared_flow])
    own, up, down = back_flow.result

    gr, grb, datt, prod = middle(pre, own, up, down, residual, cotangent, gains, attn_full)
    mine_last, other_last, grad_tokens, mine_late, other_late = attend_back(
        jnp.concatenate([seq_lengths, core.astype(jnp.int32)]), normed_first, attn_full,
        cosine, sine, tokens, gains, q, k, v, datt, lse, gr, grb, att, prod, devices // groups // 2,
    )
    mine_last, other_last, grad_tokens, mine_late, other_late = advance(
        [out_flow, in_flow, down_flow, shared_flow],
        (mine_last, other_last, grad_tokens, mine_late, other_late),
    )
    blocks = lambda array: array.reshape(
        devices // groups // 2, LINE, 2, share, array.shape[1]
    )
    last_flow = Flow(home_steps(blocks(mine_last), blocks(other_last)))
    late_flow = Flow(home_steps(blocks(mine_late), blocks(other_late), split=False))
    for flow in (last_flow, late_flow, out_flow, in_flow, down_flow, shared_flow):
        finish(flow)
    late = late_flow.result
    last, shares = last_flow.result, shared_flow.result
    block_out = layer_sum
    for part in out_flow.result:
        block_out = block_out + part.astype(F32)
    block_out = block_out.astype(BF)
    share_in, share_down = shares[:, : 2 * shared_width], shares[:share_out, 2 * shared_width :]
    share_qkv = (
        last[:, : 3 * width]
        .reshape(share, width // PAIR, 3, PAIR)
        .transpose(0, 2, 1, 3)
        .reshape(share, 3 * width)
    )

    all_ids = jnp.stack([g[rows : rows + TOP, :rows] for g in grads])
    counts = jnp.sum(
        (all_ids[None] == jnp.arange(experts_total, dtype=BF)[:, None, None, None]).astype(F32),
        axis=(1, 2, 3),
    )
    counts = jnp.broadcast_to(counts[:, None], (experts_total, HEAD_DIM))
    step = 1
    while step < devices // groups:
        counts = counts + lax.ppermute(
            counts, "dp", [(i, i ^ step) for i in range(devices // groups)]
        )
        step *= 2
    return (
        block_out, grad_tokens, share_qkv, late[:, :width], share_in, share_down,
        late[:, width], late[:, width + 1], in_flow.result, down_flow.result,
        counts[:, 0].astype(jnp.int32),
    )


def solution(mesh):
    rows = P(BOTH, None)
    flat = P(BOTH)
    experts = P("expert", None, None)
    return jax.shard_map(
        on_device,
        mesh=mesh,
        in_specs=(
            rows, rows, rows, rows, rows, flat, flat, experts, experts, rows, rows, flat, rows,
        ),
        out_specs=(
            rows, rows, rows, rows, rows, rows, flat, flat, experts, experts, P(),
        ),
        check_vma=False,
    )
```

```python
import functools

import jax
import jax.numpy as jnp
from jax import lax
from jax.experimental import pallas as pl
from jax.experimental.pallas import tpu as pltpu
from jax.sharding import PartitionSpec as P

HEADS = 10
HEAD_DIM = 128
TOP = 6
PAIR = 2 * HEAD_DIM
ROUTE_ROWS = 16
norm_eps = 1e-06

BF = jnp.bfloat16
F32 = jnp.float32
BOTH = ("dp", "expert")
together = lax.optimization_barrier


def dot(left, right, left_dim=1, right_dim=0):
    return lax.dot_general(
        left, right, (((left_dim,), (right_dim,)), ((), ())), preferred_element_type=F32
    )


def add(left, right):
    return (left.astype(F32) + right.astype(F32)).astype(BF)


def norm_scale(activation):
    return lax.rsqrt(jnp.mean(activation * activation, axis=-1, keepdims=True) + norm_eps)


def full_block(*shape):
    return pl.BlockSpec(
        shape, lambda *i: (0,) * len(shape), pipeline_mode=pl.Buffered(1)
    )


def shaped(*shape, dtype=BF):
    return jax.ShapeDtypeStruct(shape, dtype)


def kernel_cost(flops, moved):
    return pl.CostEstimate(flops=flops, bytes_accessed=moved, transcendentals=0)


def rotary_tables(row_count):
    half = HEAD_DIM // 2
    frequencies = 10000.0 ** (-(2.0 * jnp.arange(half, dtype=F32)) / HEAD_DIM)
    angles = jnp.arange(row_count).astype(F32)[:, None] * frequencies[None, :]
    cosine, sine = jnp.cos(angles), jnp.sin(angles)
    return (
        jnp.concatenate([cosine, cosine], axis=1),
        jnp.concatenate([-sine, sine], axis=1),
    )


def turn(head, cosine, sine):
    return head * cosine + pltpu.roll(head, HEAD_DIM // 2, 1) * sine


def turn_back(head, cosine, sine):
    return head * cosine - pltpu.roll(head, HEAD_DIM // 2, 1) * sine


def allowed_keys(start, stop, length):
    shape = (stop - start, stop)
    row = lax.broadcasted_iota(jnp.int32, shape, 0) + start
    column = lax.broadcasted_iota(jnp.int32, shape, 1)
    return (column <= row) & (column < length)


def attend_body(
    length_ref, wq_ref, wk_ref, wv_ref, wo_ref, gains_in_ref, cos_ref, sin_ref, tokens_ref,
    q_ref, k_ref, v_ref, att_ref, lse_ref, normed_ref, gains_ref, residual_ref, normed_second_ref,
    total_ref,
):
    step = pl.program_id(0)
    row_count = tokens_ref.shape[0]

    @pl.when(step == 0)
    def _():
        shape = (gains_ref.shape[0], HEAD_DIM)
        pick = lax.broadcasted_iota(jnp.int32, shape, 0) == lax.broadcasted_iota(
            jnp.int32, shape, 1
        )
        gains = dot(jnp.where(pick, 1.0, 0.0).astype(BF), gains_in_ref[...], 1, 1)
        gains_ref[...] = gains
        value = tokens_ref[...].astype(F32)
        normed_ref[...] = (value * norm_scale(value) * gains[0:1]).astype(BF)
        total_ref[...] = value

    normed = normed_ref[...]
    length = length_ref[0]
    cosine, sine = cos_ref[...], sin_ref[...]
    queries, keys = dot(normed, wq_ref[...]), dot(normed, wk_ref[...])
    v_ref[...] = dot(normed, wv_ref[...]).astype(BF)
    for head in range(2):
        here = slice(head * HEAD_DIM, (head + 1) * HEAD_DIM)
        q = turn(queries[:, here], cosine, sine).astype(BF)
        k = turn(keys[:, here], cosine, sine).astype(BF)
        q_ref[:, here] = q
        k_ref[:, here] = k
        for start in range(0, row_count, row_count // 2):
            stop = start + row_count // 2
            scores = dot(q[start:stop], k[:stop], 1, 1) * HEAD_DIM ** (-0.5)
            scores = jnp.where(allowed_keys(start, stop, length), scores, -1e30)
            peak = jnp.max(scores, axis=1, keepdims=True)
            weights = jnp.exp(scores - peak)
            whole = jnp.sum(weights, axis=1, keepdims=True)
            lse_ref[0, start:stop, head : head + 1] = peak + jnp.log(whole)
            att_ref[start:stop, here] = dot(
                (weights * (1.0 / whole)).astype(BF), v_ref[:stop, here]
            ).astype(BF)

    total_ref[...] += dot(att_ref[...], wo_ref[...])

    @pl.when(step == pl.num_programs(0) - 1)
    def _():
        residual = total_ref[...]
        residual_ref[...] = residual
        normed_second_ref[...] = (residual * norm_scale(residual) * gains_ref[1:2]).astype(BF)


def attend(length, weights, cosine, sine, tokens):
    rows, width = tokens.shape
    steps = width // PAIR
    part = lambda offset: pl.BlockSpec((width, PAIR), lambda i: (0, i + offset))
    pair = pl.BlockSpec((rows, PAIR), lambda i: (0, i))
    whole = full_block(rows, width)
    return pl.pallas_call(
        attend_body,
        grid=(steps,),
        in_specs=[
            pl.BlockSpec(memory_space=pltpu.SMEM),
            part(0),
            part(steps),
            part(2 * steps),
            pl.BlockSpec((PAIR, width), lambda i: (i, 3)),
            pl.BlockSpec((width, HEAD_DIM), lambda i: (0, 4 * HEADS), pipeline_mode=pl.Buffered(1)),
            full_block(rows, HEAD_DIM),
            full_block(rows, HEAD_DIM),
            whole,
        ],
        out_specs=[pair] * 4
        + [
            pl.BlockSpec((1, rows, 2), lambda i: (i, 0, 0)),
            whole,
            full_block(8, width),
            whole,
            whole,
        ],
        out_shape=[shaped(rows, width)] * 4
        + [
            shaped(steps, rows, 2, dtype=F32), shaped(rows, width), shaped(8, width, dtype=F32),
            shaped(rows, width, dtype=F32), shaped(rows, width),
        ],
        scratch_shapes=[pltpu.VMEM((rows, width), F32)],
        compiler_params=pltpu.CompilerParams(vmem_limit_bytes=48 * 2**20),
        cost_estimate=kernel_cost(10_000_000_000, 25_000_000),
        name="attend",
    )(length, weights, weights, weights, weights, weights, cosine, sine, tokens)


def middle_body(
    pre_ref, own_ref, one_ref, two_ref, residual_ref, cot_ref, gain_ref, wo_ref,
    gr_ref, grb_ref, datt_ref, prod_ref,
):
    @pl.when(pl.program_id(0) == 0)
    def _():
        value = residual_ref[...]
        scale = norm_scale(value)
        grad = pre_ref[...] + (
            own_ref[...].astype(F32) + one_ref[...].astype(F32) + two_ref[...].astype(F32)
        )
        weighted = grad * gain_ref[1:2]
        out = cot_ref[...].astype(F32) + (
            scale * weighted
            - value * (scale * scale * scale) * jnp.mean(weighted * value, axis=1, keepdims=True)
        )
        gr_ref[...] = out
        grb_ref[...] = out.astype(BF)
        prod_ref[...] = (grad * value * scale).astype(BF)

    datt_ref[...] = dot(grb_ref[...], wo_ref[...], 1, 1).astype(BF)


def middle(pre, own, one, two, residual, cot, gain, weights):
    rows, width = residual.shape
    steps = width // PAIR
    pair = pl.BlockSpec((rows, PAIR), lambda i: (0, i))
    whole = full_block(rows, width)
    return pl.pallas_call(
        middle_body,
        grid=(steps,),
        in_specs=[whole] * 6
        + [full_block(8, width), pl.BlockSpec((PAIR, width), lambda i: (i, 3))],
        out_specs=[whole, whole, pair, whole],
        out_shape=[
            shaped(rows, width, dtype=F32), shaped(rows, width), shaped(rows, width),
            shaped(rows, width),
        ],
        compiler_params=pltpu.CompilerParams(vmem_limit_bytes=48 * 2**20),
        cost_estimate=kernel_cost(4_000_000_000, 25_000_000),
        name="middle",
    )(pre, own, one, two, residual, cot, gain, weights)


def attend_back_body(
    length_ref, normed_ref, wq_ref, wk_ref, wv_ref, cos_ref, sin_ref, tokens_ref, gain_ref,
    q_ref, k_ref, v_ref, datt_ref, lse_ref, gr_ref, grb_ref, att_ref, prod_ref,
    mine_ref, other_ref, gtok_ref, mine_late_ref, other_late_ref,
    g3_ref, total_ref, turned_ref, *, chips,
):
    step = pl.program_id(0)
    normed = normed_ref[...]
    row_count, width = normed.shape
    length, core = length_ref[0], length_ref[1]
    cosine, sine = cos_ref[...], sin_ref[...]
    scale = HEAD_DIM ** (-0.5)
    unit = width // (2 * chips)

    def store(refs, columns, block):
        for mine in range(2):

            @pl.when(core == mine)
            def _(mine=mine):
                for n in range(2 * chips):
                    ref = refs[0] if n % 2 == mine else refs[1]
                    ref[n // 2 * unit : (n // 2 + 1) * unit, columns] = block(
                        slice(n * unit, (n + 1) * unit)
                    ).astype(BF)

    half = row_count // 2
    for head in range(2):
        here = slice(head * HEAD_DIM, (head + 1) * HEAD_DIM)
        grad_keys, grad_values = [], []
        for start in (0, half):
            stop = start + half
            q, k = q_ref[start:stop, here], k_ref[:stop, here]
            grad = datt_ref[start:stop, here]
            scores = dot(q, k, 1, 1) * scale
            scores = jnp.where(allowed_keys(start, stop, length), scores, -1e30)
            probs = jnp.exp(scores - lse_ref[0, start:stop, head : head + 1])
            grad_probs = dot(grad, v_ref[:stop, here], 1, 1)
            delta = jnp.sum(grad_probs * probs, axis=1, keepdims=True)
            grad_scores = (probs * (grad_probs - delta)).astype(BF)
            grad_values.append(dot(probs.astype(BF), grad, 0, 0))
            g3_ref[start:stop, here] = turn_back(
                dot(grad_scores, k) * scale, cosine[start:stop], sine[start:stop]
            ).astype(BF)
            grad_keys.append(dot(grad_scores, q, 0, 0) * scale)
        for n, (first, second) in enumerate((grad_keys, grad_values)):
            whole = jnp.concatenate([first + second[:half], second[half:]], axis=0)
            if n == 0:
                whole = turn_back(whole, cosine, sine)
            there = (n + 1) * PAIR + head * HEAD_DIM
            g3_ref[:, there : there + HEAD_DIM] = whole.astype(BF)

    @pl.when(step == 0)
    def _():
        total_ref[...] = jnp.zeros_like(total_ref)
        turned_ref[...] = normed.astype(F32).T.astype(BF)

    refs = (mine_ref, other_ref)
    columns = pl.ds(pl.multiple_of(step * 3 * PAIR, PAIR), 3 * PAIR)
    store(refs, columns, lambda some: dot(turned_ref[some], g3_ref[...]))
    total = total_ref[...]
    for n, w_ref in enumerate((wq_ref, wk_ref, wv_ref)):
        total = total + dot(g3_ref[:, n * PAIR : (n + 1) * PAIR], w_ref[...], 1, 1)
    total_ref[...] = total

    @pl.when(step == pl.num_programs(0) - 1)
    def _():
        value = tokens_ref[...].astype(F32)
        r = norm_scale(value)
        grad = total_ref[...]
        weighted = grad * gain_ref[0:1]
        gtok_ref[...] = gr_ref[...] + (
            r * weighted
            - value * (r * r * r) * jnp.mean(weighted * value, axis=1, keepdims=True)
        )
        lane = lax.broadcasted_iota(jnp.int32, (row_count, HEAD_DIM), 1)
        first = jnp.where(lane == 0, 1.0, 0.0).astype(BF)
        second = jnp.where(lane == 1, 1.0, 0.0).astype(BF)
        refs = (mine_late_ref, other_late_ref)
        gain_grads = dot((grad * value * r).astype(BF), first, 0, 0) + dot(
            prod_ref[...], second, 0, 0
        )
        store(refs, slice(width, width + HEAD_DIM), lambda some: gain_grads[some])
        turned_ref[...] = att_ref[...].astype(F32).T.astype(BF)
        store(refs, slice(0, width), lambda some: dot(turned_ref[some], grb_ref[...]))


def attend_back(
    length, normed, weights, cosine, sine, tokens, gain, q, k, v, datt, lse, gr, grb, att, prod, chips
):
    rows, width = tokens.shape
    steps = width // PAIR
    part = lambda offset: pl.BlockSpec((width, PAIR), lambda i: (0, i + offset))
    pair = pl.BlockSpec((rows, PAIR), lambda i: (0, i))
    whole = full_block(rows, width)
    return pl.pallas_call(
        functools.partial(attend_back_body, chips=chips),
        grid=(steps,),
        in_specs=[
            pl.BlockSpec(memory_space=pltpu.SMEM),
            whole,
            part(0),
            part(steps),
            part(2 * steps),
            full_block(rows, HEAD_DIM),
            full_block(rows, HEAD_DIM),
            whole,
            full_block(8, width),
            pair, pair, pair, pair,
            pl.BlockSpec((1, rows, 2), lambda i: (i, 0, 0)),
            whole, whole, whole, whole,
        ],
        out_specs=[full_block(width // 2, 3 * width)] * 2
        + [whole]
        + [full_block(width // 2, width + HEAD_DIM)] * 2,
        out_shape=[shaped(width // 2, 3 * width)] * 2
        + [shaped(rows, width, dtype=F32)]
        + [shaped(width // 2, width + HEAD_DIM)] * 2,
        scratch_shapes=[
            pltpu.VMEM((rows, 3 * PAIR), BF),
            pltpu.VMEM((rows, width), F32),
            pltpu.VMEM((width, rows), BF),
        ],
        compiler_params=pltpu.CompilerParams(vmem_limit_bytes=56 * 2**20),
        cost_estimate=kernel_cost(14_000_000_000, 40_000_000),
        name="attend_back",
    )(
        length, normed, weights, weights, weights, cosine, sine, tokens, gain,
        q, k, v, datt, lse, gr, grb, att, prod,
    )


def expert_body(mine_ref, *refs, count, capacity, hidden):
    rows_refs, grads_refs, route_refs = [refs[n * count : (n + 1) * count] for n in range(3)]
    win_hbm, wout_hbm = refs[3 * count : 3 * count + 2]
    win_ref, wout_ref, sems = refs[-3:]
    refs = refs[:-3]
    pdx_refs, pout_refs = refs[-2 * count - 4 : -count - 4], refs[-count - 4 : -4]
    x_ref, h_ref, gr_ref, dgu_ref = refs[-4:]
    step = pl.program_id(0)
    experts = win_ref.shape[0]
    copies = [
        [
            pltpu.make_async_copy(hbm.at[e], ref.at[e], sems.at[e, n])
            for n, (hbm, ref) in enumerate(((win_hbm, win_ref), (wout_hbm, wout_ref)))
        ]
        for e in range(experts)
    ]

    @pl.when(step == 0)
    def _():
        for copy in sum(copies, []):
            copy.start()

    def arrived(copy):
        @pl.when(step == 0)
        def _():
            copy.wait()

    rows, grads, routes = [g[0][...] for g in (rows_refs, grads_refs, route_refs)]
    for n in range(1, count):
        rows = jnp.where(step == n, rows_refs[n][...], rows)
        grads = jnp.where(step == n, grads_refs[n][...], grads)
        routes = jnp.where(step == n, route_refs[n][...], routes)
    row_count = rows.shape[0]
    routes = routes.astype(F32)
    ids = routes[:TOP, :row_count]
    gates = (
        routes[:TOP, row_count : 2 * row_count]
        + routes[TOP : 2 * TOP, :row_count]
        + routes[TOP : 2 * TOP, row_count : 2 * row_count]
    )
    square = (row_count, row_count)
    earlier = lax.broadcasted_iota(jnp.int32, square, 0) < lax.broadcasted_iota(
        jnp.int32, square, 1
    )
    earlier = jnp.where(earlier, 1.0, 0.0).astype(BF)
    slot = lax.broadcasted_iota(jnp.int32, (capacity, row_count), 0)
    picks, back_rows, results = [], [], []
    for e in range(experts):
        chosen = ids == (mine_ref[0] + e).astype(F32)
        named = jnp.sum(jnp.where(chosen, 1.0, 0.0), axis=0, keepdims=True)
        gate = jnp.sum(jnp.where(chosen, gates, 0.0), axis=0, keepdims=True)
        rank = dot(jnp.broadcast_to(named, (16, row_count)).astype(BF), earlier)[0:1]
        mask = slot == jnp.where(named > 0.5, rank, -1.0).astype(jnp.int32)
        pick = jnp.where(mask, 1.0, 0.0).astype(BF)
        gate_col = jnp.sum(jnp.where(mask, gate, 0.0), axis=1, keepdims=True)
        x = dot(pick, rows).astype(BF)
        x_ref[e, 0] = x
        gr = (dot(pick, grads) * gate_col).astype(BF)
        gr_ref[e, 0] = gr
        arrived(copies[e][0])
        gate_up = dot(x, win_ref[e])
        a, b = gate_up[:, :hidden], gate_up[:, hidden:]
        s = jax.nn.sigmoid(a)
        swish = a * s
        h = (swish * b).astype(BF)
        h_ref[e, 0] = h
        arrived(copies[e][1])
        gh = dot(gr, wout_ref[e], 1, 1)
        dgu_ref[e, 0, :, :hidden] = (gh * b * s * (1.0 + a * (1.0 - s))).astype(BF)
        dgu_ref[e, 0, :, hidden:] = (gh * swish).astype(BF)
        back_rows.append(dot(dgu_ref[e, 0], win_ref[e], 1, 1).astype(BF))
        results.append((dot(h, wout_ref[e]) * gate_col).astype(BF))
        picks.append(pick)
    picks = jnp.concatenate(picks, axis=0)
    back = dot(picks, jnp.concatenate(back_rows, axis=0), 0, 0).astype(BF)
    out = dot(picks, jnp.concatenate(results, axis=0), 0, 0).astype(BF)
    for n in range(count):

        @pl.when(step == n)
        def _(n=n):
            pdx_refs[n][...] = back
            pout_refs[n][...] = out


def expert_rows(first, mine, groups, rows, grads, w_in, w_out, capacity, so_far):
    count = len(rows)
    row_count, width = rows[0].shape
    experts, hidden, _ = w_out.shape
    whole = full_block(row_count, width)
    routes = pl.BlockSpec(
        (ROUTE_ROWS, width),
        lambda i, mine: (row_count // ROUTE_ROWS, 0),
        pipeline_mode=pl.Buffered(1),
    )
    slots = lambda w: pl.BlockSpec((experts, 1, capacity, w), lambda i, mine: (0, first + i, 0, 0))
    widths = (width, hidden, width, 2 * hidden)
    so_far = [] if so_far is None else list(so_far)
    out = pl.pallas_call(
        functools.partial(expert_body, count=count, capacity=capacity, hidden=hidden),
        grid_spec=pltpu.PrefetchScalarGridSpec(
            num_scalar_prefetch=1,
            grid=(count,),
            in_specs=[whole] * (2 * count)
            + [routes] * count
            + [pl.BlockSpec(memory_space=pl.ANY)] * (2 + len(so_far)),
            out_specs=[whole] * (2 * count)
            + [slots(w) for w in widths],
            scratch_shapes=[
                pltpu.VMEM(w_in.shape, BF),
                pltpu.VMEM(w_out.shape, BF),
                pltpu.SemaphoreType.DMA((experts, 2)),
            ],
        ),
        out_shape=[shaped(row_count, width)] * (2 * count)
        + [shaped(experts, groups, capacity, w) for w in widths],
        input_output_aliases={3 + 3 * count + n: 2 * count + n for n in range(len(so_far))},
        compiler_params=pltpu.CompilerParams(vmem_limit_bytes=60 * 2**20),
        cost_estimate=kernel_cost(count * 9_300_000_000, count * 8_000_000 + 14_000_000),
        name="expert_rows",
    )(mine, *rows, *grads, *grads, w_in, w_out, *so_far)
    return list(out[:count]), list(out[count : 2 * count]), list(out[2 * count :])


def expert_grads_body(core_ref, left_ref, right_ref, mine_ref, other_ref):
    merge = lambda ref: ref[0].reshape(-1, ref.shape[-1])
    grads = dot(merge(left_ref), merge(right_ref), 0, 0).astype(BF)

    @pl.when(pl.program_id(0) == 0)
    def _():
        mine_ref[...] = grads

    @pl.when(pl.program_id(0) == 1)
    def _():
        other_ref[...] = grads


def expert_grads(core, left, right, columns):
    experts, groups, capacity, width = left.shape
    steps = right.shape[3] // columns
    take = lambda w, pick: pl.BlockSpec((1, groups, capacity, w), pick)
    block = lambda pick: pl.BlockSpec((width, columns), pick)
    return pl.pallas_call(
        expert_grads_body,
        grid_spec=pltpu.PrefetchScalarGridSpec(
            num_scalar_prefetch=1,
            grid=(experts, steps),
            in_specs=[
                take(width, lambda e, i, core: ((e + core[0]) % 2, 0, 0, 0)),
                take(columns, lambda e, i, core: ((e + core[0]) % 2, 0, 0, i)),
            ],
            out_specs=[
                block(lambda e, i, core: (0, jnp.where(e == 0, i, steps - 1))),
                block(lambda e, i, core: (0, jnp.where(e == 0, 0, i))),
            ],
        ),
        out_shape=[shaped(width, right.shape[3])] * 2,
        compiler_params=pltpu.CompilerParams(vmem_limit_bytes=60 * 2**20),
        cost_estimate=kernel_cost(
            2 * experts * groups * capacity * width * right.shape[3], 40_000_000
        ),
        name="expert_grads",
    )(core, left, right)


def both_experts_body(core_ref, mine_ref, other_ref, out_ref):
    out_ref[core_ref[0]] = mine_ref[...].astype(F32)
    out_ref[1 - core_ref[0]] = other_ref[...].astype(F32)


def both_experts(core, mine, other):
    rows, width = mine.shape
    step = rows // 7 if rows % 112 == 0 else rows // 8
    block = pl.BlockSpec((step, width), lambda i, core: (i, 0))
    return pl.pallas_call(
        both_experts_body,
        grid_spec=pltpu.PrefetchScalarGridSpec(
            num_scalar_prefetch=1,
            grid=(rows // step,),
            in_specs=[block, block],
            out_specs=pl.BlockSpec((2, step, width), lambda i, core: (0, i, 0)),
        ),
        out_shape=shaped(2, rows, width, dtype=F32),
        cost_estimate=kernel_cost(rows * width, 12 * rows * width),
        name="both_experts",
    )(core, mine, other)


def shared_body(
    normed_ref, cot_ref, residual_ref, win_ref, wout_ref,
    pre_ref, sum_ref, gin_ref, gout_ref, grad_ref, *, hidden,
):
    normed, cot = normed_ref[...], cot_ref[...]
    gate_up = dot(normed, win_ref[...])
    a, b = gate_up[:, :hidden], gate_up[:, hidden:]
    s = jax.nn.sigmoid(a)
    swish = a * s
    h = (swish * b).astype(BF)
    gh = dot(cot, wout_ref[...], 1, 1)
    grad_ref[:, :hidden] = (gh * b * s * (1.0 + a * (1.0 - s))).astype(BF)
    grad_ref[:, hidden:] = (gh * swish).astype(BF)
    pre_ref[...] = dot(grad_ref[...], win_ref[...], 1, 1)
    sum_ref[...] = residual_ref[...] + dot(h, wout_ref[...])
    gin_ref[...] = dot(normed, grad_ref[...], 0, 0).astype(BF)
    gout_ref[...] = dot(h, cot, 0, 0).astype(BF)


def shared_expert(normed, cot, residual, w_in, w_out):
    rows, width = normed.shape
    hidden = w_out.shape[0]
    whole = full_block(rows, width)
    return pl.pallas_call(
        functools.partial(shared_body, hidden=hidden),
        grid=(1,),
        in_specs=[
            whole, whole, whole, full_block(width, 2 * hidden), full_block(hidden, width),
        ],
        out_specs=[whole, whole, full_block(width, 2 * hidden), full_block(hidden, width)],
        out_shape=[
            shaped(rows, width, dtype=F32), shaped(rows, width, dtype=F32),
            shaped(width, 2 * hidden), shaped(hidden, width),
        ],
        scratch_shapes=[pltpu.VMEM((rows, 2 * hidden), BF)],
        compiler_params=pltpu.CompilerParams(vmem_limit_bytes=56 * 2**20),
        cost_estimate=kernel_cost(14_000_000_000, 25_000_000),
        name="shared_expert",
    )(normed, cot, residual, w_in, w_out)


LINE = 4


def across(array):
    return lax.ppermute(array, "expert", [(i, i ^ 1) for i in range(2 * LINE)])


def along(array, hops):
    return lax.ppermute(
        array, "expert", [(2 * a + side, 2 * b + side) for a, b in hops for side in (0, 1)]
    )


def by_place(place, options):
    result = options[-1]
    for n in range(len(options) - 2, -1, -1):
        result = jnp.where(place == n, options[n], result)
    return result


class Flow:
    def __init__(self, steps):
        self.steps, self.result = steps, None
        self.waiting = next(steps)

    def feed(self, arrived):
        try:
            self.waiting = self.steps.send(arrived)
        except StopIteration as stop:
            self.waiting, self.result = (), stop.value


def advance(flows, done=()):
    arrived, done = together((tuple(f.waiting for f in flows), done))
    for flow, block in zip(flows, arrived):
        flow.feed(block)
    return done


def finish(flow):
    while flow.result is None:
        advance([flow])
    return flow.result


def gather_steps(own, place, slots):
    slots.append(own)
    y0, d1, u1 = yield (
        across(own),
        along(own, [(1, 0), (2, 1), (3, 2)]),
        along(own, [(0, 1), (1, 2), (2, 3)]),
    )
    s1 = jnp.where(place <= 1, d1, u1)
    slots += [y0, s1]
    y1, d2, u2 = yield (
        across(s1),
        along(d1, [(1, 0), (2, 1)]),
        along(u1, [(1, 2), (2, 3)]),
    )
    s2 = by_place(place, [d2, u1, d1, u2])
    slots += [y1, s2]
    y2, ud3 = yield (across(s2), along(jnp.where(place == 2, u2, d2), [(2, 3), (1, 0)]))
    s3 = by_place(place, [ud3, d2, u2, ud3])
    slots += [y2, s3]
    (y3,) = yield (across(s3),)
    slots.append(y3)
    return slots


def outer_sums(place, s2, r2, s3, t3):
    s2, s3 = s2 + r2, s3 + t3
    return jnp.where(place == 0, s2, s3), jnp.where(place == LINE - 1, s2, s3), s2


def inner_sums(place, s1, r1, s2, up, down):
    s1 = s1 + r1
    m1 = s1 + jnp.where(place == 1, up, down)
    m2 = s2 + jnp.where(place == 1, down, up)
    return by_place(place, [s1, m1, m2]), by_place(place, [m2, m2, m1, s1])


def by_rows(function, place, results, *arrays):
    rows, width = arrays[0].shape
    block = pl.BlockSpec((rows // 4, width), lambda i, place: (i, 0))

    def body(place_ref, *refs):
        values = [ref[...].astype(F32) for ref in refs[:-results]]
        for ref, value in zip(refs[-results:], function(place_ref[0], *values)):
            ref[...] = value.astype(BF)

    return pl.pallas_call(
        body,
        grid_spec=pltpu.PrefetchScalarGridSpec(
            num_scalar_prefetch=1,
            grid=(4,),
            in_specs=[block] * len(arrays),
            out_specs=[block] * results,
        ),
        out_shape=[shaped(rows, width)] * results,
        cost_estimate=kernel_cost(
            8 * rows * width, 2 * rows * width * (len(arrays) + results)
        ),
        name=function.__name__,
    )(place[None], *arrays)


def reduce_steps(place, parts):
    own, y0, s1, y1, s2, y2, s3, y3 = parts
    (r3,) = yield (across(y3),)
    s3 = add(s3, r3)
    r2, t3 = yield (across(y2), along(s3, [(0, 1), (3, 2)]))
    up, down, s2 = by_rows(outer_sums, place, 3, s2, r2, s3, t3)
    r1, up, down = yield (
        across(y1), along(up, [(0, 1), (1, 2)]), along(down, [(3, 2), (2, 1)])
    )
    up, down = by_rows(inner_sums, place, 2, s1, r1, s2, up, down)
    r0, up, down = yield (
        across(y0),
        along(up, [(0, 1), (1, 2), (2, 3)]),
        along(down, [(3, 2), (2, 1), (1, 0)]),
    )
    return add(own, r0), up, down


def pick_half(array, bit, dim):
    return lax.dynamic_index_in_dim(array, bit, dim, keepdims=False)


def split_core(count):
    return [(i, i ^ 1) for i in range(count)]


def home_steps(mine, other, split=True):
    count = lax.axis_size("dp")
    chip = lax.axis_index("dp") // 2
    place, side = lax.axis_index("expert") // 2, lax.axis_index("expert") % 2
    columns = mine.shape[-1]
    (got,) = yield (lax.ppermute(other, "dp", split_core(count)),)
    total = add(mine, got)

    def over_side(part):
        (got,) = yield (across(pick_half(part, 1 - side, 2)),)
        return add(pick_half(part, side, 2), got)

    def over_chips(part):
        while part.shape[0] > 1:
            half = part.shape[0] // 2
            bit = chip // half % 2
            part = part.reshape((2, half) + part.shape[1:])
            (got,) = yield (
                lax.ppermute(
                    pick_half(part, 1 - bit, 0), "dp", [(i, i ^ (2 * half)) for i in range(count)]
                ),
            )
            part = add(pick_half(part, bit, 0), got)
        return part

    if split:
        cut = columns // 256 * 128
        parts = [total[..., :cut], total[..., cut:]]
        rounds = ((over_side, over_chips), (over_chips, over_side))
    else:
        parts, rounds = [total], ((over_chips,), (over_side,))
    for kinds in rounds:
        flows = [Flow(kind(part)) for kind, part in zip(kinds, parts)]
        while any(f.result is None for f in flows):
            open_flows = [f for f in flows if f.result is None]
            arrived = yield tuple(f.waiting for f in open_flows)
            for flow, block in zip(open_flows, arrived):
                flow.feed(block)
        parts = [f.result for f in flows]
    part = jnp.concatenate([p[0] for p in parts], axis=-1)
    result = pick_half(part, place, 0).astype(F32)
    arrived = yield tuple(
        along(
            pick_half(part, (place + hop) % LINE, 0), [(n, (n + hop) % LINE) for n in range(LINE)]
        )
        for hop in range(1, LINE)
    )
    for block in arrived:
        result = result + block.astype(F32)
    return result


def dp_sum_steps(mine, other, core, pieces):
    count = lax.axis_size("dp")
    (got,) = yield (lax.ppermute(other, "dp", split_core(count)),)
    unit = mine.shape[0] // pieces
    done = []
    for n in range(pieces):
        piece = add(mine[n * unit : (n + 1) * unit], got[n * unit : (n + 1) * unit])
        step = 2
        while step < count:
            (there,) = yield (lax.ppermute(piece, "dp", [(i, i ^ step) for i in range(count)]),)
            piece = add(piece, there)
            step *= 2
        done.append(piece)
    total = jnp.concatenate(done, axis=0)
    (got,) = yield (lax.ppermute(total, "dp", split_core(count)),)
    return both_experts(core, total, got)


def on_device(
    tokens, w_qkv, w_attn_out, w_shared_in, w_shared_out, gain_attn, gain_ffn,
    w_expert_in, w_expert_out, route_ids, route_gates, seq_lengths, cotangent,
):
    rows, width = tokens.shape
    groups = lax.axis_size("expert")
    devices = groups * lax.axis_size("dp")
    experts = w_expert_in.shape[0]
    experts_total = experts * groups
    capacity = rows * TOP * 5 // (4 * experts_total)
    share, share_out = w_qkv.shape[0], w_shared_out.shape[0]
    shared_width = share_out * devices
    place, side = lax.axis_index("expert") // 2, lax.axis_index("expert") % 2

    live = jnp.arange(rows) < seq_lengths[0]
    ids = jnp.where(live[:, None], route_ids, -1).astype(F32).T
    own_counts = jnp.sum(
        (ids[None] == jnp.arange(experts_total, dtype=F32)[:, None, None]).astype(jnp.int32),
        axis=(1, 2),
    )
    count_rows = jnp.pad(
        jnp.stack([own_counts % 256, own_counts // 256]), ((0, share - 2), (0, 0))
    ).astype(BF)
    extra = jnp.concatenate([gain_attn[:, None], gain_ffn[:, None], count_rows], axis=1)
    gain_columns = jnp.pad(extra, ((0, 0), (0, HEAD_DIM - extra.shape[1])))
    attn_full = lax.all_gather(
        jnp.concatenate([w_qkv, w_attn_out, gain_columns], axis=1), BOTH, axis=0, tiled=True
    )
    high = lax.reduce_precision(route_gates.T, 8, 7)
    middle_bits = lax.reduce_precision(route_gates.T - high, 8, 7)
    low = route_gates.T - high - middle_bits
    routes = jnp.concatenate(
        [jnp.concatenate([ids, high], axis=1), jnp.concatenate([middle_bits, low], axis=1)], axis=0
    )
    routes = jnp.pad(
        routes, ((0, ROUTE_ROWS - 2 * TOP), (0, width - 2 * rows))
    ).astype(BF)
    grads = []
    grads_flow = Flow(
        gather_steps(jnp.concatenate([cotangent, routes], axis=0), place, grads)
    )
    mine = lax.axis_index("expert")[None] * experts
    cosine, sine = rotary_tables(rows)
    advance([grads_flow])
    advance([grads_flow])

    attended = attend(seq_lengths, attn_full, cosine, sine, tokens)
    q, k, v, att, lse, normed_first, gains, residual, normed_second = attended
    advance([grads_flow], normed_second)

    arrived, back, out, kept = [], [], [], [None]
    rows_flow = Flow(gather_steps(normed_second, place, arrived))

    def through():
        first = len(back)
        new_back, new_out, kept[0] = expert_rows(
            first, mine, groups, arrived[first:], grads[first : len(arrived)],
            w_expert_in, w_expert_out, capacity, kept[0],
        )
        back.extend(new_back)
        out.extend(new_out)

    shares_in = jnp.concatenate(
        [w_shared_in, jnp.pad(w_shared_out, ((0, share - share_out), (0, 0)))], axis=1
    )
    shared_full = None
    through()
    while rows_flow.result is None:
        more = [f for f in (grads_flow,) if f.result is None]
        back[:], out[:], kept[0], shares_in = advance(
            [rows_flow] + more, (back, out, kept[0], shares_in)
        )
        through()
        if shared_full is None and len(arrived) > 5:
            shared_full = lax.all_gather(shares_in, BOTH, axis=0, tiled=True)
    x, hidden, result_grad, gate_up_grad = kept[0]

    back_flow = Flow(reduce_steps(place, back))
    core = lax.axis_index("dp")[None] % 2
    grad_down = expert_grads(core, hidden, result_grad, width)
    grad_down, x, out = advance([back_flow], (grad_down, x, out))
    down_flow = Flow(dp_sum_steps(*grad_down, core, 1))
    grad_in = expert_grads(core, x, gate_up_grad, shared_width)
    shared_out_full = (
        shared_full[:, 2 * shared_width :]
        .reshape(devices, share, width)[:, :share_out]
        .reshape(shared_width, width)
    )
    out_flow = Flow(reduce_steps(place, out))
    grad_in, shared_full, shared_out_full = advance(
        [back_flow, down_flow], (grad_in, shared_full, shared_out_full)
    )
    in_flow = Flow(dp_sum_steps(*grad_in, core, 2))
    pre, layer_sum, grad_shared_in, grad_shared_out = advance(
        [back_flow, in_flow, down_flow, out_flow],
        shared_expert(normed_second, cotangent, residual, shared_full, shared_out_full),
    )

    def of_core(which):
        part = lambda array: pick_half(
            array.reshape(devices // groups // 2, 2, LINE, 2, -1, array.shape[1]), which, 1
        )
        below = ((0, 0),) * 3 + ((0, share - share_out), (0, 0))
        return jnp.concatenate(
            [part(grad_shared_in), jnp.pad(part(grad_shared_out), below)], axis=-1
        )

    shared_flow = Flow(home_steps(of_core(core[0]), of_core(1 - core[0]), split=False))
    advance([back_flow, in_flow])
    own, up, down = back_flow.result

    gr, grb, datt, prod = middle(pre, own, up, down, residual, cotangent, gains, attn_full)
    mine_last, other_last, grad_tokens, mine_late, other_late = attend_back(
        jnp.concatenate([seq_lengths, core.astype(jnp.int32)]), normed_first, attn_full,
        cosine, sine, tokens, gains, q, k, v, datt, lse, gr, grb, att, prod, devices // groups // 2,
    )
    mine_last, other_last, grad_tokens, mine_late, other_late = advance(
        [out_flow, in_flow, down_flow, shared_flow],
        (mine_last, other_last, grad_tokens, mine_late, other_late),
    )
    blocks = lambda array: array.reshape(
        devices // groups // 2, LINE, 2, share, array.shape[1]
    )
    last_flow = Flow(home_steps(blocks(mine_last), blocks(other_last)))
    late_flow = Flow(home_steps(blocks(mine_late), blocks(other_late), split=False))
    for flow in (last_flow, late_flow, out_flow, in_flow, down_flow, shared_flow):
        finish(flow)
    late = late_flow.result
    last, shares = last_flow.result, shared_flow.result
    block_out = layer_sum
    for part in out_flow.result:
        block_out = block_out + part.astype(F32)
    block_out = block_out.astype(BF)
    share_in, share_down = shares[:, : 2 * shared_width], shares[:share_out, 2 * shared_width :]
    share_qkv = (
        last[:, : 3 * width]
        .reshape(share, width // PAIR, 3, PAIR)
        .transpose(0, 2, 1, 3)
        .reshape(share, 3 * width)
    )

    digits = attn_full[:, 4 * width + 2 : 4 * width + 2 + experts_total].astype(F32)
    digits = jnp.sum(digits.reshape(devices, share, experts_total)[:, :2], axis=0)
    counts = (digits[0] + 256.0 * digits[1]).astype(jnp.int32)
    return (
        block_out, grad_tokens, share_qkv, late[:, :width], share_in, share_down,
        late[:, width], late[:, width + 1], in_flow.result, down_flow.result,
        counts,
    )


def solution(mesh):
    rows = P(BOTH, None)
    flat = P(BOTH)
    experts = P("expert", None, None)
    return jax.shard_map(
        on_device,
        mesh=mesh,
        in_specs=(
            rows, rows, rows, rows, rows, flat, flat, experts, experts, rows, rows, flat, rows,
        ),
        out_specs=(
            rows, rows, rows, rows, rows, rows, flat, flat, experts, experts, P(),
        ),
        check_vma=False,
    )
```

```python
import functools

import jax
import jax.numpy as jnp
from jax import lax
from jax.experimental import pallas as pl
from jax.experimental.pallas import tpu as pltpu
from jax.sharding import PartitionSpec as P

HEADS = 10
HEAD_DIM = 128
TOP = 6
PAIR = 2 * HEAD_DIM
ROUTE_ROWS = 16
norm_eps = 1e-06

BF = jnp.bfloat16
F32 = jnp.float32
BOTH = ("dp", "expert")
together = lax.optimization_barrier


def dot(left, right, left_dim=1, right_dim=0):
    return lax.dot_general(
        left, right, (((left_dim,), (right_dim,)), ((), ())), preferred_element_type=F32
    )


def add(left, right):
    return (left.astype(F32) + right.astype(F32)).astype(BF)


def norm_scale(activation):
    return lax.rsqrt(jnp.mean(activation * activation, axis=-1, keepdims=True) + norm_eps)


def full_block(*shape):
    return pl.BlockSpec(
        shape, lambda *i: (0,) * len(shape), pipeline_mode=pl.Buffered(1)
    )


def shaped(*shape, dtype=BF):
    return jax.ShapeDtypeStruct(shape, dtype)


def kernel_cost(flops, moved):
    return pl.CostEstimate(flops=flops, bytes_accessed=moved, transcendentals=0)


def rotary_tables(row_count):
    half = HEAD_DIM // 2
    frequencies = 10000.0 ** (-(2.0 * jnp.arange(half, dtype=F32)) / HEAD_DIM)
    angles = jnp.arange(row_count).astype(F32)[:, None] * frequencies[None, :]
    cosine, sine = jnp.cos(angles), jnp.sin(angles)
    return (
        jnp.concatenate([cosine, cosine], axis=1),
        jnp.concatenate([-sine, sine], axis=1),
    )


def turn(head, cosine, sine):
    return head * cosine + pltpu.roll(head, HEAD_DIM // 2, 1) * sine


def turn_back(head, cosine, sine):
    return head * cosine - pltpu.roll(head, HEAD_DIM // 2, 1) * sine


def allowed_keys(start, stop, length):
    shape = (stop - start, stop)
    row = lax.broadcasted_iota(jnp.int32, shape, 0) + start
    column = lax.broadcasted_iota(jnp.int32, shape, 1)
    return (column <= row) & (column < length)


def attend_body(
    length_ref, wq_ref, wk_ref, wv_ref, wo_ref, gains_in_ref, cos_ref, sin_ref, tokens_ref,
    q_ref, k_ref, v_ref, att_ref, lse_ref, normed_ref, gains_ref, residual_ref, normed_second_ref,
    total_ref,
):
    step = pl.program_id(0)
    row_count = tokens_ref.shape[0]

    @pl.when(step == 0)
    def _():
        shape = (gains_ref.shape[0], HEAD_DIM)
        pick = lax.broadcasted_iota(jnp.int32, shape, 0) == lax.broadcasted_iota(
            jnp.int32, shape, 1
        )
        gains = dot(jnp.where(pick, 1.0, 0.0).astype(BF), gains_in_ref[...], 1, 1)
        gains_ref[...] = gains
        value = tokens_ref[...].astype(F32)
        normed_ref[...] = (value * norm_scale(value) * gains[0:1]).astype(BF)
        total_ref[...] = value

    normed = normed_ref[...]
    length = length_ref[0]
    cosine, sine = cos_ref[...], sin_ref[...]
    queries, keys = dot(normed, wq_ref[...]), dot(normed, wk_ref[...])
    v_ref[...] = dot(normed, wv_ref[...]).astype(BF)
    for head in range(2):
        here = slice(head * HEAD_DIM, (head + 1) * HEAD_DIM)
        q = turn(queries[:, here], cosine, sine).astype(BF)
        k = turn(keys[:, here], cosine, sine).astype(BF)
        q_ref[:, here] = q
        k_ref[:, here] = k
        for start in range(0, row_count, row_count // 2):
            stop = start + row_count // 2
            scores = dot(q[start:stop], k[:stop], 1, 1) * HEAD_DIM ** (-0.5)
            scores = jnp.where(allowed_keys(start, stop, length), scores, -1e30)
            peak = jnp.max(scores, axis=1, keepdims=True)
            weights = jnp.exp(scores - peak)
            whole = jnp.sum(weights, axis=1, keepdims=True)
            lse_ref[0, start:stop, head : head + 1] = peak + jnp.log(whole)
            att_ref[start:stop, here] = dot(
                (weights * (1.0 / whole)).astype(BF), v_ref[:stop, here]
            ).astype(BF)

    total_ref[...] += dot(att_ref[...], wo_ref[...])

    @pl.when(step == pl.num_programs(0) - 1)
    def _():
        residual = total_ref[...]
        residual_ref[...] = residual
        normed_second_ref[...] = (residual * norm_scale(residual) * gains_ref[1:2]).astype(BF)


def attend(length, weights, cosine, sine, tokens):
    rows, width = tokens.shape
    steps = width // PAIR
    part = lambda offset: pl.BlockSpec((width, PAIR), lambda i: (0, i + offset))
    pair = pl.BlockSpec((rows, PAIR), lambda i: (0, i))
    whole = full_block(rows, width)
    return pl.pallas_call(
        attend_body,
        grid=(steps,),
        in_specs=[
            pl.BlockSpec(memory_space=pltpu.SMEM),
            part(0),
            part(steps),
            part(2 * steps),
            pl.BlockSpec((PAIR, width), lambda i: (i, 3)),
            pl.BlockSpec((width, HEAD_DIM), lambda i: (0, 4 * HEADS), pipeline_mode=pl.Buffered(1)),
            full_block(rows, HEAD_DIM),
            full_block(rows, HEAD_DIM),
            whole,
        ],
        out_specs=[pair] * 4
        + [
            pl.BlockSpec((1, rows, 2), lambda i: (i, 0, 0)),
            whole,
            full_block(8, width),
            whole,
            whole,
        ],
        out_shape=[shaped(rows, width)] * 4
        + [
            shaped(steps, rows, 2, dtype=F32), shaped(rows, width), shaped(8, width, dtype=F32),
            shaped(rows, width, dtype=F32), shaped(rows, width),
        ],
        scratch_shapes=[pltpu.VMEM((rows, width), F32)],
        compiler_params=pltpu.CompilerParams(vmem_limit_bytes=48 * 2**20),
        cost_estimate=kernel_cost(10_000_000_000, 25_000_000),
        name="attend",
    )(length, weights, weights, weights, weights, weights, cosine, sine, tokens)


def middle_body(
    pre_ref, own_ref, one_ref, two_ref, residual_ref, cot_ref, gain_ref, wo_ref,
    gr_ref, grb_ref, datt_ref, prod_ref,
):
    @pl.when(pl.program_id(0) == 0)
    def _():
        value = residual_ref[...]
        scale = norm_scale(value)
        grad = pre_ref[...] + (
            own_ref[...].astype(F32) + one_ref[...].astype(F32) + two_ref[...].astype(F32)
        )
        weighted = grad * gain_ref[1:2]
        out = cot_ref[...].astype(F32) + (
            scale * weighted
            - value * (scale * scale * scale) * jnp.mean(weighted * value, axis=1, keepdims=True)
        )
        gr_ref[...] = out
        grb_ref[...] = out.astype(BF)
        prod_ref[...] = (grad * value * scale).astype(BF)

    datt_ref[...] = dot(grb_ref[...], wo_ref[...], 1, 1).astype(BF)


def middle(pre, own, one, two, residual, cot, gain, weights):
    rows, width = residual.shape
    steps = width // PAIR
    pair = pl.BlockSpec((rows, PAIR), lambda i: (0, i))
    whole = full_block(rows, width)
    return pl.pallas_call(
        middle_body,
        grid=(steps,),
        in_specs=[whole] * 6
        + [full_block(8, width), pl.BlockSpec((PAIR, width), lambda i: (i, 3))],
        out_specs=[whole, whole, pair, whole],
        out_shape=[
            shaped(rows, width, dtype=F32), shaped(rows, width), shaped(rows, width),
            shaped(rows, width),
        ],
        compiler_params=pltpu.CompilerParams(vmem_limit_bytes=48 * 2**20),
        cost_estimate=kernel_cost(4_000_000_000, 25_000_000),
        name="middle",
    )(pre, own, one, two, residual, cot, gain, weights)


def attend_back_body(
    length_ref, normed_ref, wq_ref, wk_ref, wv_ref, cos_ref, sin_ref, tokens_ref, gain_ref,
    q_ref, k_ref, v_ref, datt_ref, lse_ref, gr_ref, grb_ref, att_ref, prod_ref,
    mine_ref, other_ref, gtok_ref, mine_late_ref, other_late_ref,
    g3_ref, total_ref, turned_ref, *, chips,
):
    step = pl.program_id(0)
    normed = normed_ref[...]
    row_count, width = normed.shape
    length, core = length_ref[0], length_ref[1]
    cosine, sine = cos_ref[...], sin_ref[...]
    scale = HEAD_DIM ** (-0.5)
    unit = width // (2 * chips)

    def store(refs, columns, block):
        for mine in range(2):

            @pl.when(core == mine)
            def _(mine=mine):
                for n in range(2 * chips):
                    ref = refs[0] if n % 2 == mine else refs[1]
                    ref[n // 2 * unit : (n // 2 + 1) * unit, columns] = block(
                        slice(n * unit, (n + 1) * unit)
                    ).astype(BF)

    half = row_count // 2
    for head in range(2):
        here = slice(head * HEAD_DIM, (head + 1) * HEAD_DIM)
        grad_keys, grad_values = [], []
        for start in (0, half):
            stop = start + half
            q, k = q_ref[start:stop, here], k_ref[:stop, here]
            grad = datt_ref[start:stop, here]
            scores = dot(q, k, 1, 1) * scale
            scores = jnp.where(allowed_keys(start, stop, length), scores, -1e30)
            probs = jnp.exp(scores - lse_ref[0, start:stop, head : head + 1])
            grad_probs = dot(grad, v_ref[:stop, here], 1, 1)
            delta = jnp.sum(grad_probs * probs, axis=1, keepdims=True)
            grad_scores = (probs * (grad_probs - delta)).astype(BF)
            grad_values.append(dot(probs.astype(BF), grad, 0, 0))
            g3_ref[start:stop, here] = turn_back(
                dot(grad_scores, k) * scale, cosine[start:stop], sine[start:stop]
            ).astype(BF)
            grad_keys.append(dot(grad_scores, q, 0, 0) * scale)
        for n, (first, second) in enumerate((grad_keys, grad_values)):
            whole = jnp.concatenate([first + second[:half], second[half:]], axis=0)
            if n == 0:
                whole = turn_back(whole, cosine, sine)
            there = (n + 1) * PAIR + head * HEAD_DIM
            g3_ref[:, there : there + HEAD_DIM] = whole.astype(BF)

    @pl.when(step == 0)
    def _():
        total_ref[...] = jnp.zeros_like(total_ref)
        turned_ref[...] = normed.astype(F32).T.astype(BF)

    refs = (mine_ref, other_ref)
    columns = pl.ds(pl.multiple_of(step * 3 * PAIR, PAIR), 3 * PAIR)
    store(refs, columns, lambda some: dot(turned_ref[some], g3_ref[...]))
    total = total_ref[...]
    for n, w_ref in enumerate((wq_ref, wk_ref, wv_ref)):
        total = total + dot(g3_ref[:, n * PAIR : (n + 1) * PAIR], w_ref[...], 1, 1)
    total_ref[...] = total

    @pl.when(step == pl.num_programs(0) - 1)
    def _():
        value = tokens_ref[...].astype(F32)
        r = norm_scale(value)
        grad = total_ref[...]
        weighted = grad * gain_ref[0:1]
        gtok_ref[...] = gr_ref[...] + (
            r * weighted
            - value * (r * r * r) * jnp.mean(weighted * value, axis=1, keepdims=True)
        )
        lane = lax.broadcasted_iota(jnp.int32, (row_count, HEAD_DIM), 1)
        first = jnp.where(lane == 0, 1.0, 0.0).astype(BF)
        second = jnp.where(lane == 1, 1.0, 0.0).astype(BF)
        refs = (mine_late_ref, other_late_ref)
        gain_grads = dot((grad * value * r).astype(BF), first, 0, 0) + dot(
            prod_ref[...], second, 0, 0
        )
        store(refs, slice(width, width + HEAD_DIM), lambda some: gain_grads[some])
        turned_ref[...] = att_ref[...].astype(F32).T.astype(BF)
        store(refs, slice(0, width), lambda some: dot(turned_ref[some], grb_ref[...]))


def attend_back(
    length, normed, weights, cosine, sine, tokens, gain, q, k, v, datt, lse, gr, grb, att, prod, chips
):
    rows, width = tokens.shape
    steps = width // PAIR
    part = lambda offset: pl.BlockSpec((width, PAIR), lambda i: (0, i + offset))
    pair = pl.BlockSpec((rows, PAIR), lambda i: (0, i))
    whole = full_block(rows, width)
    return pl.pallas_call(
        functools.partial(attend_back_body, chips=chips),
        grid=(steps,),
        in_specs=[
            pl.BlockSpec(memory_space=pltpu.SMEM),
            whole,
            part(0),
            part(steps),
            part(2 * steps),
            full_block(rows, HEAD_DIM),
            full_block(rows, HEAD_DIM),
            whole,
            full_block(8, width),
            pair, pair, pair, pair,
            pl.BlockSpec((1, rows, 2), lambda i: (i, 0, 0)),
            whole, whole, whole, whole,
        ],
        out_specs=[full_block(width // 2, 3 * width)] * 2
        + [whole]
        + [full_block(width // 2, width + HEAD_DIM)] * 2,
        out_shape=[shaped(width // 2, 3 * width)] * 2
        + [shaped(rows, width, dtype=F32)]
        + [shaped(width // 2, width + HEAD_DIM)] * 2,
        scratch_shapes=[
            pltpu.VMEM((rows, 3 * PAIR), BF),
            pltpu.VMEM((rows, width), F32),
            pltpu.VMEM((width, rows), BF),
        ],
        compiler_params=pltpu.CompilerParams(vmem_limit_bytes=56 * 2**20),
        cost_estimate=kernel_cost(14_000_000_000, 40_000_000),
        name="attend_back",
    )(
        length, normed, weights, weights, weights, cosine, sine, tokens, gain,
        q, k, v, datt, lse, gr, grb, att, prod,
    )


def expert_body(mine_ref, *refs, count, capacity, hidden):
    rows_refs, grads_refs, route_refs = [refs[n * count : (n + 1) * count] for n in range(3)]
    win_hbm, wout_hbm = refs[3 * count : 3 * count + 2]
    win_ref, wout_ref, sems = refs[-3:]
    refs = refs[:-3]
    pdx_refs, pout_refs = refs[-2 * count - 4 : -count - 4], refs[-count - 4 : -4]
    x_ref, h_ref, gr_ref, dgu_ref = refs[-4:]
    step = pl.program_id(0)
    experts = win_ref.shape[0]
    copies = [
        [
            pltpu.make_async_copy(hbm.at[e], ref.at[e], sems.at[e, n])
            for n, (hbm, ref) in enumerate(((win_hbm, win_ref), (wout_hbm, wout_ref)))
        ]
        for e in range(experts)
    ]

    @pl.when(step == 0)
    def _():
        for copy in sum(copies, []):
            copy.start()

    def arrived(copy):
        @pl.when(step == 0)
        def _():
            copy.wait()

    rows, grads, routes = [g[0][...] for g in (rows_refs, grads_refs, route_refs)]
    for n in range(1, count):
        rows = jnp.where(step == n, rows_refs[n][...], rows)
        grads = jnp.where(step == n, grads_refs[n][...], grads)
        routes = jnp.where(step == n, route_refs[n][...], routes)
    row_count = rows.shape[0]
    routes = routes.astype(F32)
    ids = routes[:TOP, :row_count]
    gates = (
        routes[:TOP, row_count : 2 * row_count]
        + routes[TOP : 2 * TOP, :row_count]
        + routes[TOP : 2 * TOP, row_count : 2 * row_count]
    )
    square = (row_count, row_count)
    earlier = lax.broadcasted_iota(jnp.int32, square, 0) < lax.broadcasted_iota(
        jnp.int32, square, 1
    )
    earlier = jnp.where(earlier, 1.0, 0.0).astype(BF)
    slot = lax.broadcasted_iota(jnp.int32, (capacity, row_count), 0)
    picks, back_rows, results = [], [], []
    for e in range(experts):
        chosen = ids == (mine_ref[0] + e).astype(F32)
        named = jnp.sum(jnp.where(chosen, 1.0, 0.0), axis=0, keepdims=True)
        gate = jnp.sum(jnp.where(chosen, gates, 0.0), axis=0, keepdims=True)
        rank = dot(jnp.broadcast_to(named, (16, row_count)).astype(BF), earlier)[0:1]
        mask = slot == jnp.where(named > 0.5, rank, -1.0).astype(jnp.int32)
        pick = jnp.where(mask, 1.0, 0.0).astype(BF)
        gate_col = jnp.sum(jnp.where(mask, gate, 0.0), axis=1, keepdims=True)
        x = dot(pick, rows).astype(BF)
        x_ref[e, 0] = x
        gr = (dot(pick, grads) * gate_col).astype(BF)
        gr_ref[e, 0] = gr
        arrived(copies[e][0])
        gate_up = dot(x, win_ref[e])
        a, b = gate_up[:, :hidden], gate_up[:, hidden:]
        s = jax.nn.sigmoid(a)
        swish = a * s
        h = (swish * b).astype(BF)
        h_ref[e, 0] = h
        arrived(copies[e][1])
        gh = dot(gr, wout_ref[e], 1, 1)
        dgu_ref[e, 0, :, :hidden] = (gh * b * s * (1.0 + a * (1.0 - s))).astype(BF)
        dgu_ref[e, 0, :, hidden:] = (gh * swish).astype(BF)
        back_rows.append(dot(dgu_ref[e, 0], win_ref[e], 1, 1).astype(BF))
        results.append((dot(h, wout_ref[e]) * gate_col).astype(BF))
        picks.append(pick)
    picks = jnp.concatenate(picks, axis=0)
    back = dot(picks, jnp.concatenate(back_rows, axis=0), 0, 0).astype(BF)
    out = dot(picks, jnp.concatenate(results, axis=0), 0, 0).astype(BF)
    for n in range(count):

        @pl.when(step == n)
        def _(n=n):
            pdx_refs[n][...] = back
            pout_refs[n][...] = out


def expert_rows(first, mine, groups, rows, grads, w_in, w_out, capacity, so_far):
    count = len(rows)
    row_count, width = rows[0].shape
    experts, hidden, _ = w_out.shape
    whole = full_block(row_count, width)
    routes = pl.BlockSpec(
        (ROUTE_ROWS, width),
        lambda i, mine: (row_count // ROUTE_ROWS, 0),
        pipeline_mode=pl.Buffered(1),
    )
    slots = lambda w: pl.BlockSpec((experts, 1, capacity, w), lambda i, mine: (0, first + i, 0, 0))
    widths = (width, hidden, width, 2 * hidden)
    so_far = [] if so_far is None else list(so_far)
    out = pl.pallas_call(
        functools.partial(expert_body, count=count, capacity=capacity, hidden=hidden),
        grid_spec=pltpu.PrefetchScalarGridSpec(
            num_scalar_prefetch=1,
            grid=(count,),
            in_specs=[whole] * (2 * count)
            + [routes] * count
            + [pl.BlockSpec(memory_space=pl.ANY)] * (2 + len(so_far)),
            out_specs=[whole] * (2 * count)
            + [slots(w) for w in widths],
            scratch_shapes=[
                pltpu.VMEM(w_in.shape, BF),
                pltpu.VMEM(w_out.shape, BF),
                pltpu.SemaphoreType.DMA((experts, 2)),
            ],
        ),
        out_shape=[shaped(row_count, width)] * (2 * count)
        + [shaped(experts, groups, capacity, w) for w in widths],
        input_output_aliases={3 + 3 * count + n: 2 * count + n for n in range(len(so_far))},
        compiler_params=pltpu.CompilerParams(vmem_limit_bytes=60 * 2**20),
        cost_estimate=kernel_cost(count * 9_300_000_000, count * 8_000_000 + 14_000_000),
        name="expert_rows",
    )(mine, *rows, *grads, *grads, w_in, w_out, *so_far)
    return list(out[:count]), list(out[count : 2 * count]), list(out[2 * count :])


def expert_grads_body(core_ref, left_ref, right_ref, mine_ref, other_ref):
    merge = lambda ref: ref[0].reshape(-1, ref.shape[-1])
    grads = dot(merge(left_ref), merge(right_ref), 0, 0).astype(BF)

    @pl.when(pl.program_id(0) == 0)
    def _():
        mine_ref[...] = grads

    @pl.when(pl.program_id(0) == 1)
    def _():
        other_ref[...] = grads


def expert_grads(core, left, right, columns):
    experts, groups, capacity, width = left.shape
    steps = right.shape[3] // columns
    take = lambda w, pick: pl.BlockSpec((1, groups, capacity, w), pick)
    block = lambda pick: pl.BlockSpec((width, columns), pick)
    return pl.pallas_call(
        expert_grads_body,
        grid_spec=pltpu.PrefetchScalarGridSpec(
            num_scalar_prefetch=1,
            grid=(experts, steps),
            in_specs=[
                take(width, lambda e, i, core: ((e + core[0]) % 2, 0, 0, 0)),
                take(columns, lambda e, i, core: ((e + core[0]) % 2, 0, 0, i)),
            ],
            out_specs=[
                block(lambda e, i, core: (0, jnp.where(e == 0, i, steps - 1))),
                block(lambda e, i, core: (0, jnp.where(e == 0, 0, i))),
            ],
        ),
        out_shape=[shaped(width, right.shape[3])] * 2,
        compiler_params=pltpu.CompilerParams(vmem_limit_bytes=60 * 2**20),
        cost_estimate=kernel_cost(
            2 * experts * groups * capacity * width * right.shape[3], 40_000_000
        ),
        name="expert_grads",
    )(core, left, right)


def both_experts_body(core_ref, mine_ref, other_ref, out_ref):
    out_ref[core_ref[0]] = mine_ref[...].astype(F32)
    out_ref[1 - core_ref[0]] = other_ref[...].astype(F32)


def both_experts(core, mine, other):
    rows, width = mine.shape
    step = rows // 7 if rows % 112 == 0 else rows // 8
    block = pl.BlockSpec((step, width), lambda i, core: (i, 0))
    return pl.pallas_call(
        both_experts_body,
        grid_spec=pltpu.PrefetchScalarGridSpec(
            num_scalar_prefetch=1,
            grid=(rows // step,),
            in_specs=[block, block],
            out_specs=pl.BlockSpec((2, step, width), lambda i, core: (0, i, 0)),
        ),
        out_shape=shaped(2, rows, width, dtype=F32),
        cost_estimate=kernel_cost(rows * width, 12 * rows * width),
        name="both_experts",
    )(core, mine, other)


def shared_body(
    normed_ref, cot_ref, residual_ref, win_ref, wout_ref,
    pre_ref, sum_ref, gin_ref, gout_ref, grad_ref, *, hidden,
):
    normed, cot = normed_ref[...], cot_ref[...]
    gate_up = dot(normed, win_ref[...])
    a, b = gate_up[:, :hidden], gate_up[:, hidden:]
    s = jax.nn.sigmoid(a)
    swish = a * s
    h = (swish * b).astype(BF)
    gh = dot(cot, wout_ref[...], 1, 1)
    grad_ref[:, :hidden] = (gh * b * s * (1.0 + a * (1.0 - s))).astype(BF)
    grad_ref[:, hidden:] = (gh * swish).astype(BF)
    pre_ref[...] = dot(grad_ref[...], win_ref[...], 1, 1)
    sum_ref[...] = residual_ref[...] + dot(h, wout_ref[...])
    gin_ref[...] = dot(normed, grad_ref[...], 0, 0).astype(BF)
    gout_ref[...] = dot(h, cot, 0, 0).astype(BF)


def shared_expert(normed, cot, residual, w_in, w_out):
    rows, width = normed.shape
    hidden = w_out.shape[0]
    whole = full_block(rows, width)
    return pl.pallas_call(
        functools.partial(shared_body, hidden=hidden),
        grid=(1,),
        in_specs=[
            whole, whole, whole, full_block(width, 2 * hidden), full_block(hidden, width),
        ],
        out_specs=[whole, whole, full_block(width, 2 * hidden), full_block(hidden, width)],
        out_shape=[
            shaped(rows, width, dtype=F32), shaped(rows, width, dtype=F32),
            shaped(width, 2 * hidden), shaped(hidden, width),
        ],
        scratch_shapes=[pltpu.VMEM((rows, 2 * hidden), BF)],
        compiler_params=pltpu.CompilerParams(vmem_limit_bytes=56 * 2**20),
        cost_estimate=kernel_cost(14_000_000_000, 25_000_000),
        name="shared_expert",
    )(normed, cot, residual, w_in, w_out)


LINE = 4


def across(array):
    return lax.ppermute(array, "expert", [(i, i ^ 1) for i in range(2 * LINE)])


def along(array, hops):
    return lax.ppermute(
        array, "expert", [(2 * a + side, 2 * b + side) for a, b in hops for side in (0, 1)]
    )


def by_place(place, options):
    result = options[-1]
    for n in range(len(options) - 2, -1, -1):
        result = jnp.where(place == n, options[n], result)
    return result


class Flow:
    def __init__(self, steps):
        self.steps, self.result = steps, None
        self.waiting = next(steps)

    def feed(self, arrived):
        try:
            self.waiting = self.steps.send(arrived)
        except StopIteration as stop:
            self.waiting, self.result = (), stop.value


def advance(flows, done=()):
    arrived, done = together((tuple(f.waiting for f in flows), done))
    for flow, block in zip(flows, arrived):
        flow.feed(block)
    return done


def finish(flow):
    while flow.result is None:
        advance([flow])
    return flow.result


def gather_steps(own, place, slots):
    slots.append(own)
    y0, d1, u1 = yield (
        across(own),
        along(own, [(1, 0), (2, 1), (3, 2)]),
        along(own, [(0, 1), (1, 2), (2, 3)]),
    )
    s1 = jnp.where(place <= 1, d1, u1)
    slots += [y0, s1]
    y1, d2, u2 = yield (
        across(s1),
        along(d1, [(1, 0), (2, 1)]),
        along(u1, [(1, 2), (2, 3)]),
    )
    s2 = by_place(place, [d2, u1, d1, u2])
    slots += [y1, s2]
    y2, ud3 = yield (across(s2), along(jnp.where(place == 2, u2, d2), [(2, 3), (1, 0)]))
    s3 = by_place(place, [ud3, d2, u2, ud3])
    slots += [y2, s3]
    (y3,) = yield (across(s3),)
    slots.append(y3)
    return slots


def outer_sums(place, s2, r2, s3, t3):
    s2, s3 = s2 + r2, s3 + t3
    return jnp.where(place == 0, s2, s3), jnp.where(place == LINE - 1, s2, s3), s2


def inner_sums(place, s1, r1, s2, up, down):
    s1 = s1 + r1
    m1 = s1 + jnp.where(place == 1, up, down)
    m2 = s2 + jnp.where(place == 1, down, up)
    return by_place(place, [s1, m1, m2]), by_place(place, [m2, m2, m1, s1])


def by_rows(function, place, results, *arrays):
    rows, width = arrays[0].shape
    block = pl.BlockSpec((rows // 4, width), lambda i, place: (i, 0))

    def body(place_ref, *refs):
        values = [ref[...].astype(F32) for ref in refs[:-results]]
        for ref, value in zip(refs[-results:], function(place_ref[0], *values)):
            ref[...] = value.astype(BF)

    return pl.pallas_call(
        body,
        grid_spec=pltpu.PrefetchScalarGridSpec(
            num_scalar_prefetch=1,
            grid=(4,),
            in_specs=[block] * len(arrays),
            out_specs=[block] * results,
        ),
        out_shape=[shaped(rows, width)] * results,
        cost_estimate=kernel_cost(
            8 * rows * width, 2 * rows * width * (len(arrays) + results)
        ),
        name=function.__name__,
    )(place[None], *arrays)


def reduce_steps(place, parts):
    own, y0, s1, y1, s2, y2, s3, y3 = parts
    (r3,) = yield (across(y3),)
    s3 = add(s3, r3)
    r2, t3 = yield (across(y2), along(s3, [(0, 1), (3, 2)]))
    up, down, s2 = by_rows(outer_sums, place, 3, s2, r2, s3, t3)
    r1, up, down = yield (
        across(y1), along(up, [(0, 1), (1, 2)]), along(down, [(3, 2), (2, 1)])
    )
    up, down = by_rows(inner_sums, place, 2, s1, r1, s2, up, down)
    r0, up, down = yield (
        across(y0),
        along(up, [(0, 1), (1, 2), (2, 3)]),
        along(down, [(3, 2), (2, 1), (1, 0)]),
    )
    return add(own, r0), up, down


def pick_half(array, bit, dim):
    return lax.dynamic_index_in_dim(array, bit, dim, keepdims=False)


def split_core(count):
    return [(i, i ^ 1) for i in range(count)]


def home_steps(mine, other, split=True):
    count = lax.axis_size("dp")
    chip = lax.axis_index("dp") // 2
    place, side = lax.axis_index("expert") // 2, lax.axis_index("expert") % 2
    columns = mine.shape[-1]
    (got,) = yield (lax.ppermute(other, "dp", split_core(count)),)
    total = add(mine, got)

    def over_side(part):
        (got,) = yield (across(pick_half(part, 1 - side, 2)),)
        return add(pick_half(part, side, 2), got)

    def over_chips(part):
        while part.shape[0] > 1:
            half = part.shape[0] // 2
            bit = chip // half % 2
            part = part.reshape((2, half) + part.shape[1:])
            (got,) = yield (
                lax.ppermute(
                    pick_half(part, 1 - bit, 0), "dp", [(i, i ^ (2 * half)) for i in range(count)]
                ),
            )
            part = add(pick_half(part, bit, 0), got)
        return part

    if split:
        cut = columns // 256 * 128
        parts = [total[..., :cut], total[..., cut:]]
        rounds = ((over_side, over_chips), (over_chips, over_side))
    else:
        parts, rounds = [total], ((over_chips,), (over_side,))
    for kinds in rounds:
        flows = [Flow(kind(part)) for kind, part in zip(kinds, parts)]
        while any(f.result is None for f in flows):
            open_flows = [f for f in flows if f.result is None]
            arrived = yield tuple(f.waiting for f in open_flows)
            for flow, block in zip(open_flows, arrived):
                flow.feed(block)
        parts = [f.result for f in flows]
    part = jnp.concatenate([p[0] for p in parts], axis=-1)
    result = pick_half(part, place, 0).astype(F32)
    arrived = yield tuple(
        along(
            pick_half(part, (place + hop) % LINE, 0), [(n, (n + hop) % LINE) for n in range(LINE)]
        )
        for hop in range(1, LINE)
    )
    for block in arrived:
        result = result + block.astype(F32)
    return result


def dp_sum_steps(mine, other, core, pieces):
    count = lax.axis_size("dp")
    (got,) = yield (lax.ppermute(other, "dp", split_core(count)),)
    unit = mine.shape[0] // pieces
    done = []
    for n in range(pieces):
        piece = add(mine[n * unit : (n + 1) * unit], got[n * unit : (n + 1) * unit])
        step = 2
        while step < count:
            (there,) = yield (lax.ppermute(piece, "dp", [(i, i ^ step) for i in range(count)]),)
            piece = add(piece, there)
            step *= 2
        done.append(piece)
    total = jnp.concatenate(done, axis=0)
    (got,) = yield (lax.ppermute(total, "dp", split_core(count)),)
    return both_experts(core, total, got)


def on_device(
    tokens, w_qkv, w_attn_out, w_shared_in, w_shared_out, gain_attn, gain_ffn,
    w_expert_in, w_expert_out, route_ids, route_gates, seq_lengths, cotangent,
):
    rows, width = tokens.shape
    groups = lax.axis_size("expert")
    devices = groups * lax.axis_size("dp")
    experts = w_expert_in.shape[0]
    experts_total = experts * groups
    capacity = rows * TOP * 5 // (4 * experts_total)
    share, share_out = w_qkv.shape[0], w_shared_out.shape[0]
    shared_width = share_out * devices
    place, side = lax.axis_index("expert") // 2, lax.axis_index("expert") % 2

    live = jnp.arange(rows) < seq_lengths[0]
    ids = jnp.where(live[:, None], route_ids, -1).astype(F32).T
    own_counts = jnp.sum(
        (ids[None] == jnp.arange(experts_total, dtype=F32)[:, None, None]).astype(jnp.int32),
        axis=(1, 2),
    )
    count_rows = jnp.pad(
        jnp.stack([own_counts % 256, own_counts // 256]), ((0, share - 2), (0, 0))
    ).astype(BF)
    extra = jnp.concatenate([gain_attn[:, None], gain_ffn[:, None], count_rows], axis=1)
    gain_columns = jnp.pad(extra, ((0, 0), (0, HEAD_DIM - extra.shape[1])))
    attn_full = lax.all_gather(
        jnp.concatenate([w_qkv, w_attn_out, gain_columns], axis=1), BOTH, axis=0, tiled=True
    )
    high = lax.reduce_precision(route_gates.T, 8, 7)
    middle_bits = lax.reduce_precision(route_gates.T - high, 8, 7)
    low = route_gates.T - high - middle_bits
    routes = jnp.concatenate(
        [jnp.concatenate([ids, high], axis=1), jnp.concatenate([middle_bits, low], axis=1)], axis=0
    )
    routes = jnp.pad(
        routes, ((0, ROUTE_ROWS - 2 * TOP), (0, width - 2 * rows))
    ).astype(BF)
    grads = []
    grads_flow = Flow(
        gather_steps(jnp.concatenate([cotangent, routes], axis=0), place, grads)
    )
    mine = lax.axis_index("expert")[None] * experts
    cosine, sine = rotary_tables(rows)
    advance([grads_flow])
    advance([grads_flow])

    attended = attend(seq_lengths, attn_full, cosine, sine, tokens)
    q, k, v, att, lse, normed_first, gains, residual, normed_second = attended
    advance([grads_flow], normed_second)

    arrived, back, out, kept = [], [], [], [None]
    rows_flow = Flow(gather_steps(normed_second, place, arrived))

    def through():
        first = len(back)
        new_back, new_out, kept[0] = expert_rows(
            first, mine, groups, arrived[first:], grads[first : len(arrived)],
            w_expert_in, w_expert_out, capacity, kept[0],
        )
        back.extend(new_back)
        out.extend(new_out)

    shares_in = jnp.concatenate(
        [w_shared_in, jnp.pad(w_shared_out, ((0, share - share_out), (0, 0)))], axis=1
    )
    shared_full = None
    through()
    while rows_flow.result is None:
        more = [f for f in (grads_flow,) if f.result is None]
        back[:], out[:], kept[0], shares_in = advance(
            [rows_flow] + more, (back, out, kept[0], shares_in)
        )
        through()
        if shared_full is None and len(arrived) > 3:
            shared_full = lax.all_gather(shares_in, BOTH, axis=0, tiled=True)
    x, hidden, result_grad, gate_up_grad = kept[0]

    back_flow = Flow(reduce_steps(place, back))
    core = lax.axis_index("dp")[None] % 2
    grad_down = expert_grads(core, hidden, result_grad, width)
    grad_down, x, out = advance([back_flow], (grad_down, x, out))
    down_flow = Flow(dp_sum_steps(*grad_down, core, 1))
    grad_in = expert_grads(core, x, gate_up_grad, shared_width)
    shared_out_full = (
        shared_full[:, 2 * shared_width :]
        .reshape(devices, share, width)[:, :share_out]
        .reshape(shared_width, width)
    )
    out_flow = Flow(reduce_steps(place, out))
    grad_in, shared_full, shared_out_full = advance(
        [back_flow, down_flow], (grad_in, shared_full, shared_out_full)
    )
    in_flow = Flow(dp_sum_steps(*grad_in, core, 2))
    pre, layer_sum, grad_shared_in, grad_shared_out = advance(
        [back_flow, in_flow, down_flow],
        shared_expert(normed_second, cotangent, residual, shared_full, shared_out_full),
    )

    def of_core(which):
        part = lambda array: pick_half(
            array.reshape(devices // groups // 2, 2, LINE, 2, -1, array.shape[1]), which, 1
        )
        below = ((0, 0),) * 3 + ((0, share - share_out), (0, 0))
        return jnp.concatenate(
            [part(grad_shared_in), jnp.pad(part(grad_shared_out), below)], axis=-1
        )

    shared_flow = Flow(home_steps(of_core(core[0]), of_core(1 - core[0]), split=False))
    advance([back_flow, in_flow, out_flow])
    own, up, down = back_flow.result

    gr, grb, datt, prod = middle(pre, own, up, down, residual, cotangent, gains, attn_full)
    mine_last, other_last, grad_tokens, mine_late, other_late = attend_back(
        jnp.concatenate([seq_lengths, core.astype(jnp.int32)]), normed_first, attn_full,
        cosine, sine, tokens, gains, q, k, v, datt, lse, gr, grb, att, prod, devices // groups // 2,
    )
    mine_last, other_last, grad_tokens, mine_late, other_late = advance(
        [out_flow, in_flow, down_flow, shared_flow],
        (mine_last, other_last, grad_tokens, mine_late, other_late),
    )
    blocks = lambda array: array.reshape(
        devices // groups // 2, LINE, 2, share, array.shape[1]
    )
    last_flow = Flow(home_steps(blocks(mine_last), blocks(other_last)))
    late_flow = Flow(home_steps(blocks(mine_late), blocks(other_late), split=False))
    for flow in (last_flow, late_flow, out_flow, in_flow, down_flow, shared_flow):
        finish(flow)
    late = late_flow.result
    last, shares = last_flow.result, shared_flow.result
    block_out = layer_sum
    for part in out_flow.result:
        block_out = block_out + part.astype(F32)
    block_out = block_out.astype(BF)
    share_in, share_down = shares[:, : 2 * shared_width], shares[:share_out, 2 * shared_width :]
    share_qkv = (
        last[:, : 3 * width]
        .reshape(share, width // PAIR, 3, PAIR)
        .transpose(0, 2, 1, 3)
        .reshape(share, 3 * width)
    )

    digits = attn_full[:, 4 * width + 2 : 4 * width + 2 + experts_total].astype(F32)
    digits = jnp.sum(digits.reshape(devices, share, experts_total)[:, :2], axis=0)
    counts = (digits[0] + 256.0 * digits[1]).astype(jnp.int32)
    return (
        block_out, grad_tokens, share_qkv, late[:, :width], share_in, share_down,
        late[:, width], late[:, width + 1], in_flow.result, down_flow.result,
        counts,
    )


def solution(mesh):
    rows = P(BOTH, None)
    flat = P(BOTH)
    experts = P("expert", None, None)
    return jax.shard_map(
        on_device,
        mesh=mesh,
        in_specs=(
            rows, rows, rows, rows, rows, flat, flat, experts, experts, rows, rows, flat, rows,
        ),
        out_specs=(
            rows, rows, rows, rows, rows, rows, flat, flat, experts, experts, P(),
        ),
        check_vma=False,
    )
```
